512 devices in a mesh: dp: 128 (over y, z, core), tensor: 4 (over x).
Axes of the slice: x: 4, y: 8, z: 8, core: 2. Of those that a mesh axis runs over, the one named last changes fastest.
Arguments:
- tokens_in: bfloat16 [75776, 256], P(('dp', 'tensor')), as said below
- grad_hidden: bfloat16 [75776, 16384], P('dp', 'tensor'), as said below
Outputs:
- decoded: float32 [256, 16384], P('dp', 'tensor')
- code_total: float32 [256, 16384], P('dp', 'tensor')
Inputs may be any that keep to these rules, and one draw needn't show every extreme that they name: `tokens_in`: features of a token, of order one. `grad_hidden`: gradients of order one over the square root of 75776.
All inputs are finite; a program needn't handle non-finite values.
Results may differ from the reference program's by a relative error of at most 0.0065.
Values may be sent and summed in bfloat16 or wider, within the bound.
A program may use at most 64 MiB of HBM per device.

```python
import math
import jax
import jax.numpy as jnp
import numpy as np
from jax import lax

TOK_DEV = 592
ROWS = 256
HID_DEV = 4096
HAD = 128
UNITS = 16384
TOKENS = 75776
N_DP = 128
N_TENSOR = 4


def draw_tokens_in(key, part):
    key = jax.random.fold_in(key, 11)
    first_key, second_key = jax.random.split(key)
    row_factor = jnp.exp(jax.random.uniform(first_key, (ROWS,), jnp.float32, math.log(0.3), math.log(3.0)))
    base = jax.random.truncated_normal(second_key, -4.0, 4.0, (TOKENS, ROWS), jnp.float32)
    return (base * row_factor[None, :]).astype(jnp.bfloat16)


def owner_order(order_key, count):
    return jax.random.permutation(order_key, count)


def draw_grad_hidden(key, part):
    key = jax.random.fold_in(key, 23)
    first_key = jax.random.fold_in(key, 0)
    second_key = jax.random.fold_in(key, 1)
    fourth_key = jax.random.fold_in(key, 3)
    groups = TOKENS // TOK_DEV
    half_width = HID_DEV // 2
    column_groups = UNITS // half_width
    order_keys = jax.random.split(fourth_key, column_groups)
    ranking = jax.vmap(owner_order, in_axes=(0, None))(order_keys, groups)
    spread = jnp.transpose(ranking).astype(jnp.float32) / max(groups - 1, 1)
    column_factor = jnp.exp(jax.random.uniform(first_key, (UNITS,), jnp.float32, math.log(0.3), math.log(3.0)))
    base = jax.random.truncated_normal(second_key, -4.0, 4.0, (TOKENS, UNITS), jnp.float32)
    rising = 3.0 ** spread
    shaped = (base * column_factor[None, :]).reshape(groups, TOK_DEV, column_groups, half_width)
    scaled = shaped * rising[:, None, :, None] * TOKENS ** (-0.5)
    return scaled.reshape(TOKENS, UNITS).astype(jnp.bfloat16)


def setup_inputs(seed: int = 0) -> dict:
    keys = jax.random.split(jax.random.key(seed), 3)
    return {
        "tokens_in": draw_tokens_in(jax.random.fold_in(keys[2], 71), 0),
        "grad_hidden": draw_grad_hidden(jax.random.fold_in(keys[2], 71), 0),
    }


epsilon = 1e-06
code_limit = 448.0
clip_ratio = 2.0

def hadamard_table(points):
    index = np.arange(points)
    both = index[:, None] & index[None, :]
    parity = np.zeros((points, points), np.int64)
    for shift in range(16):
        parity = parity + (both >> shift & 1)
    return (np.where(parity % 2 == 0, 1.0, -1.0) / np.sqrt(points)).astype(np.float32)

def rotate_rows(partial_value):
    table = jnp.asarray(hadamard_table(HAD), jnp.float32)
    rows, width = partial_value.shape
    blocks = partial_value.reshape(rows, width // HAD, HAD)
    turned = jnp.einsum('rbk,kj->rbj', blocks, table, precision=lax.Precision.HIGHEST)
    return turned.reshape(rows, width)

def rotated_part(inputs, grads):
    partial_value = lax.dot_general(inputs, grads, (((0,), (0,)), ((), ())), preferred_element_type=jnp.float32)
    return rotate_rows(partial_value)

def reference(tokens_in, grad_hidden):
    inputs = tokens_in.reshape(N_DP, TOK_DEV, ROWS)
    grads = grad_hidden.reshape(N_DP, TOK_DEV, UNITS)
    groups = 2 * N_TENSOR
    half_width = HID_DEV // 2

    def peak_step(carry, pair):
        rotated = rotated_part(pair[0], pair[1])
        squares = lax.optimization_barrier(jnp.mean(jnp.square(rotated).reshape(ROWS, groups, half_width), axis=2))
        local = jnp.sqrt(squares + epsilon)
        return (jnp.maximum(carry, local), None)
    row_peak, _ = lax.scan(peak_step, jnp.zeros((ROWS, groups), jnp.float32), (inputs, grads))
    row_scale = clip_ratio * row_peak / code_limit
    wide_scale = jnp.repeat(row_scale, half_width, axis=1)

    def code_step(total, pair):
        rotated = rotated_part(pair[0], pair[1])
        coded = jnp.clip(rotated / wide_scale, -code_limit, code_limit).astype(jnp.bfloat16)
        return (total + coded.astype(jnp.float32), None)
    summed, _ = lax.scan(code_step, jnp.zeros((ROWS, UNITS), jnp.float32), (inputs, grads))
    return (summed * wide_scale, summed / code_limit)
```

```python
import jax
import jax.numpy as jnp
from jax import lax
from jax.experimental import pallas as pl
from jax.experimental.pallas import tpu as pltpu
from jax.sharding import PartitionSpec as P

NY = 8
NZ = 8
NT = 4
TOKENS = 148
STEP = 144
SLOT = 160
DEPTH = 592
ROWS = 256
HALF = 128
HID = 4096
GROUP = 2048
EPS = 1e-06
F32 = jnp.float32
BF16 = jnp.bfloat16
MESH = pl.DeviceIdType.MESH
FAR_FIRST = (4, 3, 5, 2, 6, 1, 7)


def row_order(group):
    new = lax.broadcasted_iota(jnp.int32, (ROWS, ROWS), 0)
    old = lax.broadcasted_iota(jnp.int32, (ROWS, ROWS), 1)
    core, first, second, i = new >> 7, (new >> 4) & 7, (new >> 1) & 7, new & 1
    y, z = (first, second) if group == 0 else (second, first)
    return jnp.where(old == 32 * y + 4 * z + 2 * core + i, 1.0, 0.0).astype(BF16)


def hadamard_pair():
    row = lax.broadcasted_iota(jnp.int32, (256, 256), 0)
    column = lax.broadcasted_iota(jnp.int32, (256, 256), 1)
    both = row & column & 127
    both = both ^ (both >> 4)
    both = both ^ (both >> 2)
    both = both ^ (both >> 1)
    sign = jnp.where((both & 1) == 0, 0.0625, -0.0625)
    return jnp.where((row >> 7) == (column >> 7), sign, 0.0).astype(BF16)


def kernel(
    tok_ref, grad_ref, dec_ref, tot_ref,
    slots, gbuf, feat, turned, part, rot, other, squares,
    qall, qfirst, q1, q2, peak, inv, code, land1, acc, w, pack, land2,
    gsem, tsend, trecv, q1send, q1recv, q2send, q2recv, xsend, xrecv,
    send1, recv1, send2, recv2,
):
    dp = lax.axis_index("dp")
    t = lax.axis_index("tensor")
    c = lax.rem(dp, 2)
    z = lax.rem(lax.div(dp, 2), NZ)
    y = lax.div(dp, 2 * NZ)
    oc = 1 - c

    def device(yy, zz, cc):
        return (yy * (2 * NZ) + zz * 2 + cc, t)

    def shift(value, k, n):
        return lax.rem(value + k, n)

    grad_copy = pltpu.make_async_copy(grad_ref, gbuf, gsem)
    grad_copy.start()

    barrier = pltpu.get_barrier_semaphore()
    peers_t = [(dp, shift(t, k, NT)) for k in range(1, NT)]
    peers_1 = [
        (kz * 2 + kc, shift(c, kc, 2), device(y, shift(z, kz, NZ), shift(c, kc, 2)))
        for kz in range(NZ)
        for kc in range(2)
        if kz + kc > 0
    ]
    peers_y = [device(shift(y, k, NY), z, c) for k in range(1, NY)]
    everyone = peers_t + [p[2] for p in peers_1] + peers_y
    for peer in everyone:
        pl.semaphore_signal(barrier, inc=1, device_id=peer, device_id_type=MESH)
    slots[t] = tok_ref[...]
    table = hadamard_pair()
    pl.semaphore_wait(barrier, len(everyone))

    token_copies = []
    for k in range(1, NT):
        copy = pltpu.make_async_remote_copy(
            src_ref=slots.at[t], dst_ref=slots.at[t],
            send_sem=tsend.at[k], recv_sem=trecv.at[t],
            device_id=(dp, shift(t, k, NT)), device_id_type=MESH,
        )
        copy.start()
        token_copies.append(copy)
    for k in range(1, NT):
        source = shift(t, k, NT)
        pltpu.make_async_remote_copy(
            src_ref=slots.at[source], dst_ref=slots.at[source],
            send_sem=tsend.at[k], recv_sem=trecv.at[source],
            device_id=(dp, source), device_id_type=MESH,
        ).wait_recv()
    feat[0:STEP, :] = slots[0, 0:STEP, :]
    for s in range(1, NT):
        feat[s * STEP:s * STEP + 16, :] = (
            slots[s - 1, STEP:SLOT, :].astype(F32) + slots[s, 0:16, :].astype(F32)
        ).astype(BF16)
        last = SLOT if s == NT - 1 else STEP
        feat[s * STEP + 16:s * STEP + last, :] = slots[s, 16:last, :]
    features = feat[...]
    for g in range(2):
        turned[g] = lax.dot_general(
            row_order(g), features, (((1,), (1,)), ((), ())), preferred_element_type=F32
        ).astype(BF16)

    grad_copy.wait()
    ones = jnp.ones((8, 128), F32)
    for g in range(2):
        left = turned[g]
        for tile in range(GROUP // 256):
            at = g * GROUP + tile * 256
            value = jnp.dot(left, gbuf[:, at:at + 256], preferred_element_type=F32)
            part[:, at:at + 256] = value
            both = value[:, :128] * value[:, :128] + value[:, 128:] * value[:, 128:]
            squares[...] = both if tile == 0 else squares[...] + both
        q = lax.dot_general(
            ones, squares[...], (((1,), (1,)), ((), ())),
            preferred_element_type=F32, precision=lax.Precision.HIGHEST,
        )
        for half in range(2):
            qall[half, g:g + 1, :] = q[0:1, half * HALF:(half + 1) * HALF]

    for slot, core, peer in peers_1:
        pltpu.make_async_remote_copy(
            src_ref=qall.at[core], dst_ref=q1.at[slot],
            send_sem=q1send, recv_sem=q1recv, device_id=peer, device_id_type=MESH,
        ).start()

    def rotate(half, g, j):
        rows = pl.ds(pl.multiple_of(half * HALF, HALF), HALF)
        at = g * GROUP + j * 1024
        value = jnp.concatenate(
            [part[rows, at + n * 256:at + (n + 1) * 256] for n in range(4)], axis=0
        )
        high = value.astype(BF16)
        low = (value - high.astype(F32)).astype(BF16)
        result = (
            jnp.dot(high, table, preferred_element_type=F32)
            + jnp.dot(low, table, preferred_element_type=F32)
        ).astype(BF16)
        for n in range(4):
            rot[g, rows, j * 1024 + n * 256:j * 1024 + (n + 1) * 256] = (
                result[n * HALF:(n + 1) * HALF]
            )

    def cross(g, j):
        return pltpu.make_async_remote_copy(
            src_ref=rot.at[g, pl.ds(pl.multiple_of(oc * HALF, HALF), HALF), pl.ds(j * 1024, 1024)],
            dst_ref=other.at[g, :, pl.ds(j * 1024, 1024)],
            send_sem=xsend.at[g * 2 + j], recv_sem=xrecv.at[g * 2 + j],
            device_id=device(y, z, oc), device_id_type=MESH,
        )

    for g in range(2):
        for j in range(2):
            rotate(oc, g, j)
            cross(g, j).start()

    q1_all = pltpu.make_async_remote_copy(
        src_ref=q1.at[pl.ds(1, 15)], dst_ref=q1.at[pl.ds(1, 15)],
        send_sem=q1send, recv_sem=q1recv, device_id=device(y, z, oc), device_id_type=MESH,
    )
    q1_all.wait_recv()
    best = qall[c]
    for slot in range(1, 16):
        best = jnp.maximum(best, q1[slot])
    qfirst[...] = best
    for k in range(1, NY):
        pltpu.make_async_remote_copy(
            src_ref=qfirst, dst_ref=q2.at[k],
            send_sem=q2send, recv_sem=q2recv, device_id=peers_y[k - 1], device_id_type=MESH,
        ).start()
    for g in range(2):
        for j in range(2):
            rotate(c, g, j)
    q2_all = pltpu.make_async_remote_copy(
        src_ref=q2.at[pl.ds(1, 7)], dst_ref=q2.at[pl.ds(1, 7)],
        send_sem=q2send, recv_sem=q2recv, device_id=peers_y[0], device_id_type=MESH,
    )
    q2_all.wait_recv()
    best = qfirst[...]
    for k in range(1, NY):
        best = jnp.maximum(best, q2[k])
    best = jnp.sqrt(best / float(GROUP) + EPS)
    for g in range(2):
        wide = jnp.transpose(jnp.broadcast_to(best[g:g + 1, :], (HALF, 128)))
        peak[g] = wide
        inv[g] = 0.7071067811865476 / wide
    for g in range(2):
        for j in range(2):
            cross(g, j).wait_recv()

    def coded(g, k):
        place = shift((y, z)[g], k, 8)
        rows = pl.ds(pl.multiple_of(place * 16, 16), 16)
        mine = pl.ds(pl.multiple_of(c * HALF + place * 16, 16), 16)
        scale = jnp.concatenate([inv[g, rows, :]] * (GROUP // 128), axis=1)
        own = jnp.clip(rot[g, mine, :].astype(F32) * scale, -1.0, 1.0)
        return own + jnp.clip(other[g, rows, :].astype(F32) * scale, -1.0, 1.0)

    def first(g, k):
        peer = device(shift(y, k, NY), z, c) if g == 0 else device(y, shift(z, k, NZ), c)
        return pltpu.make_async_remote_copy(
            src_ref=code.at[g, k], dst_ref=land1.at[g, k],
            send_sem=send1.at[g, k], recv_sem=recv1.at[g, k],
            device_id=peer, device_id_type=MESH,
        )

    for k in FAR_FIRST:
        for g in range(2):
            code[g, k] = coded(g, k).astype(BF16)
            first(g, k).start()
    for g in range(2):
        acc[g] = coded(g, 0)

    def second(g, k):
        peer = device(y, shift(z, k, NZ), c) if g == 0 else device(shift(y, k, NY), z, c)
        return pltpu.make_async_remote_copy(
            src_ref=pack.at[g, shift((z, y)[g], k, 8)], dst_ref=land2.at[g, k],
            send_sem=send2.at[g, k], recv_sem=recv2.at[g, k],
            device_id=peer, device_id_type=MESH,
        )

    for k in FAR_FIRST:
        for g in range(2):
            first(g, k).wait_recv()
            acc[g] = acc[g] + land1[g, k].astype(F32)
    for g in range(2):
        for block in range(16):
            w[g, block * 16:(block + 1) * 16, :] = acc[g, :, block * 128:(block + 1) * 128]
        for place in range(8):
            pack[g, place] = jnp.concatenate(
                [w[g, pl.ds(place * 2 + i, 16, stride=16), :] for i in range(2)], axis=0
            ).astype(BF16)
        for k in FAR_FIRST:
            second(g, k).start()

    for g in range(2):
        total = pack[g, (z, y)[g]].astype(F32)
        for k in FAR_FIRST:
            second(g, k).wait_recv()
            total = total + land2[g, k].astype(F32)
        for i in range(2):
            row = (y, z)[g] * 16 + (z, y)[g] * 2 + i
            value = total[i * 16:(i + 1) * 16]
            at = i * 32 + g * 16
            tot_ref[at:at + 16, :] = value
            dec_ref[at:at + 16, :] = value * (2.0 * peak[g, pl.ds(row, 1), :])

    for copy in token_copies:
        copy.wait_send()
    q1_all.wait_send()
    q2_all.wait_send()
    for g in range(2):
        for j in range(2):
            cross(g, j).wait_send()
        for k in FAR_FIRST:
            first(g, k).wait_send()
            second(g, k).wait_send()


def local(tokens_in, grad_hidden):
    start = 4 * lax.axis_index("tensor")
    slot = lax.dynamic_update_slice(
        jnp.zeros((SLOT, ROWS), BF16), tokens_in, (start, jnp.zeros_like(start))
    )
    dma = pltpu.SemaphoreType.DMA
    decoded, total = pl.pallas_call(
        kernel,
        out_shape=[jax.ShapeDtypeStruct((64, 128), F32)] * 2,
        in_specs=[
            pl.BlockSpec(memory_space=pltpu.VMEM),
            pl.BlockSpec(memory_space=pl.ANY),
        ],
        out_specs=[pl.BlockSpec(memory_space=pltpu.VMEM)] * 2,
        scratch_shapes=[
            pltpu.VMEM((NT, SLOT, ROWS), BF16),
            pltpu.VMEM((DEPTH, HID), BF16),
            pltpu.VMEM((DEPTH, ROWS), BF16),
            pltpu.VMEM((2, ROWS, DEPTH), BF16),
            pltpu.VMEM((ROWS, HID), F32),
            pltpu.VMEM((2, ROWS, GROUP), BF16),
            pltpu.VMEM((2, HALF, GROUP), BF16),
            pltpu.VMEM((ROWS, 128), F32),
            pltpu.VMEM((2, 2, 128), F32),
            pltpu.VMEM((2, 128), F32),
            pltpu.VMEM((16, 2, 128), F32),
            pltpu.VMEM((8, 2, 128), F32),
            pltpu.VMEM((2, HALF, 128), F32),
            pltpu.VMEM((2, HALF, 128), F32),
            pltpu.VMEM((2, 8, 16, GROUP), BF16),
            pltpu.VMEM((2, 8, 16, GROUP), BF16),
            pltpu.VMEM((2, 16, GROUP), F32),
            pltpu.VMEM((2, 256, 128), F32),
            pltpu.VMEM((2, 8, 32, 128), BF16),
            pltpu.VMEM((2, 8, 32, 128), BF16),
            dma, dma((NT,)), dma((NT,)), dma, dma, dma, dma, dma((4,)), dma((4,)),
            dma((2, 8)), dma((2, 8)), dma((2, 8)), dma((2, 8)),
        ],
        compiler_params=pltpu.CompilerParams(
            collective_id=0, has_side_effects=True, vmem_limit_bytes=48 * 1024 * 1024
        ),
        cost_estimate=pl.CostEstimate(
            flops=2 * DEPTH * ROWS * HID, bytes_accessed=2 * DEPTH * HID, transcendentals=0
        ),
    )(slot, grad_hidden)
    return decoded.reshape(2, HID), total.reshape(2, HID)


def solution(mesh):
    placed = (P(("dp", "tensor"), None), P("dp", "tensor"))
    return jax.shard_map(
        local,
        mesh=mesh,
        in_specs=placed,
        out_specs=(P("dp", "tensor"), P("dp", "tensor")),
        check_vma=False,
    )
```

```python
import jax
import jax.numpy as jnp
from jax import lax
from jax.experimental import pallas as pl
from jax.experimental.pallas import tpu as pltpu
from jax.sharding import PartitionSpec as P

NY = 8
NZ = 8
NT = 4
TOKENS = 148
STEP = 144
SLOT = 160
DEPTH = 592
ROWS = 256
HALF = 128
HID = 4096
GROUP = 2048
EPS = 1e-06
F32 = jnp.float32
BF16 = jnp.bfloat16
MESH = pl.DeviceIdType.MESH
FAR_FIRST = (4, 3, 5, 2, 6, 1, 7)
TARGETS = (-4, -3, 3, -1, 1, 2, -2)
HOPS = (-2, -1, 1, -1, 1, 2, -2)


def row_order(group):
    new = lax.broadcasted_iota(jnp.int32, (ROWS, ROWS), 0)
    old = lax.broadcasted_iota(jnp.int32, (ROWS, ROWS), 1)
    core, first, second, i = new >> 7, (new >> 4) & 7, (new >> 1) & 7, new & 1
    y, z = (first, second) if group == 0 else (second, first)
    return jnp.where(old == 32 * y + 4 * z + 2 * core + i, 1.0, 0.0).astype(BF16)


def hadamard_pair():
    row = lax.broadcasted_iota(jnp.int32, (256, 256), 0)
    column = lax.broadcasted_iota(jnp.int32, (256, 256), 1)
    both = row & column & 127
    both = both ^ (both >> 4)
    both = both ^ (both >> 2)
    both = both ^ (both >> 1)
    sign = jnp.where((both & 1) == 0, 0.0625, -0.0625)
    return jnp.where((row >> 7) == (column >> 7), sign, 0.0).astype(BF16)


def kernel(
    tok_ref, grad_ref, dec_ref, tot_ref,
    shifted, table, slots, gbuf, turned, part, rot, other, squares,
    qall, qfirst, q1, q2, peak, inv, code, land1, acc, w, pack, land2,
    gsem, tsend, trecv, q1send, q1recv, q2send, q2recv, xsend, xrecv,
    send1, recv1, send2, recv2,
):
    dp = lax.axis_index("dp")
    t = lax.axis_index("tensor")
    c = lax.rem(dp, 2)
    z = lax.rem(lax.div(dp, 2), NZ)
    y = lax.div(dp, 2 * NZ)
    oc = 1 - c

    def device(yy, zz, cc):
        return (yy * (2 * NZ) + zz * 2 + cc, t)

    def shift(value, k, n):
        return lax.rem(value + k, n)

    barrier = pltpu.get_barrier_semaphore()
    peers_t = [(dp, shift(t, k, NT)) for k in range(1, NT)]
    peers_1 = [
        (kz * 2 + kc, shift(c, kc, 2), device(y, shift(z, kz, NZ), shift(c, kc, 2)))
        for kz in range(NZ)
        for kc in range(2)
        if kz + kc > 0
    ]
    peers_y = [device(shift(y, k, NY), z, c) for k in range(1, NY)]
    everyone = peers_t + [p[2] for p in peers_1] + peers_y
    for peer in everyone:
        pl.semaphore_signal(barrier, inc=1, device_id=peer, device_id_type=MESH)
    grad_copy = pltpu.make_async_copy(grad_ref, gbuf, gsem)
    grad_copy.start()
    table[...] = hadamard_pair()
    shifted[...] = jnp.zeros((SLOT, ROWS), F32)
    shifted[0:TOKENS, :] = tok_ref[...].astype(F32)
    slots[0] = pltpu.roll(shifted[...], 4 * t, 0).astype(BF16)
    pl.semaphore_wait(barrier, len(everyone))

    def tokens(k):
        return pltpu.make_async_remote_copy(
            src_ref=slots.at[0], dst_ref=slots.at[k],
            send_sem=tsend.at[k], recv_sem=trecv.at[k],
            device_id=(dp, shift(t, k, NT)), device_id_type=MESH,
        )

    for k in (1, 3, 2):
        tokens(k).start()
    squares[...] = jnp.zeros_like(squares)
    for k in (0, 1, 3, 2):
        source = shift(t, NT - k, NT)
        if k > 0:
            tokens(k).wait_recv()
        features = slots[k]
        for g in range(2):
            turned[g] = lax.dot_general(
                row_order(g), features, (((1,), (1,)), ((), ())), preferred_element_type=F32
            ).astype(BF16)
        if k == 0:
            grad_copy.wait()
        depth = pl.ds(pl.multiple_of(source * STEP, 16), SLOT)

        def columns(n, carry):
            g = lax.div(n, 2)
            left = turned[g]
            for tile in range(4):
                at = pl.ds(pl.multiple_of(n * 1024 + tile * 256, 256), 256)
                value = jnp.dot(left, gbuf[depth, at], preferred_element_type=F32)
                if k > 0:
                    value = part[:, at] + value
                part[:, at] = value
                if k == 2:
                    both = value * value
                    squares[g] = squares[g] + (both[:, :128] + both[:, 128:])
            return carry

        lax.fori_loop(0, 4, columns, 0)
    ones = jnp.ones((8, 128), F32)
    for g in range(2):
        q = lax.dot_general(
            ones, squares[g], (((1,), (1,)), ((), ())),
            preferred_element_type=F32, precision=lax.Precision.HIGHEST,
        )
        for half in range(2):
            qall[half, g:g + 1, :] = q[0:1, half * HALF:(half + 1) * HALF]

    for slot, core, peer in peers_1:
        pltpu.make_async_remote_copy(
            src_ref=qall.at[core], dst_ref=q1.at[slot],
            send_sem=q1send, recv_sem=q1recv, device_id=peer, device_id_type=MESH,
        ).start()

    def rotate(half, n):
        g, j = lax.div(n, 2), lax.rem(n, 2)
        rows = pl.ds(pl.multiple_of(half * HALF, HALF), HALF)
        value = jnp.concatenate(
            [
                part[rows, pl.ds(pl.multiple_of(n * 1024 + m * 256, 256), 256)]
                for m in range(4)
            ],
            axis=0,
        )
        high = value.astype(BF16)
        low = (value - high.astype(F32)).astype(BF16)
        result = (
            jnp.dot(high, table[...], preferred_element_type=F32)
            + jnp.dot(low, table[...], preferred_element_type=F32)
        ).astype(BF16)
        for m in range(4):
            at = pl.ds(pl.multiple_of(j * 1024 + m * 256, 256), 256)
            rot[g, rows, at] = result[m * HALF:(m + 1) * HALF]

    def cross(n):
        g, at = lax.div(n, 2), pl.ds(pl.multiple_of(lax.rem(n, 2) * 1024, 1024), 1024)
        return pltpu.make_async_remote_copy(
            src_ref=rot.at[g, pl.ds(pl.multiple_of(oc * HALF, HALF), HALF), at],
            dst_ref=other.at[g, :, at],
            send_sem=xsend.at[n], recv_sem=xrecv.at[n],
            device_id=device(y, z, oc), device_id_type=MESH,
        )

    def rotate_theirs(n, carry):
        rotate(oc, n)
        cross(n).start()
        return carry

    def rotate_mine(n, carry):
        rotate(c, n)
        return carry

    lax.fori_loop(0, 4, rotate_theirs, 0)

    q1_all = pltpu.make_async_remote_copy(
        src_ref=q1.at[pl.ds(1, 15)], dst_ref=q1.at[pl.ds(1, 15)],
        send_sem=q1send, recv_sem=q1recv, device_id=device(y, z, oc), device_id_type=MESH,
    )
    q1_all.wait_recv()
    best = qall[c]
    for slot in range(1, 16):
        best = jnp.maximum(best, q1[slot])
    qfirst[...] = best
    for k in range(1, NY):
        pltpu.make_async_remote_copy(
            src_ref=qfirst, dst_ref=q2.at[k],
            send_sem=q2send, recv_sem=q2recv, device_id=peers_y[k - 1], device_id_type=MESH,
        ).start()
    lax.fori_loop(0, 4, rotate_mine, 0)
    q2_all = pltpu.make_async_remote_copy(
        src_ref=q2.at[pl.ds(1, 7)], dst_ref=q2.at[pl.ds(1, 7)],
        send_sem=q2send, recv_sem=q2recv, device_id=peers_y[0], device_id_type=MESH,
    )
    q2_all.wait_recv()
    best = qfirst[...]
    for k in range(1, NY):
        best = jnp.maximum(best, q2[k])
    best = jnp.sqrt(best / float(GROUP) + EPS)
    for g in range(2):
        wide = jnp.transpose(jnp.broadcast_to(best[g:g + 1, :], (HALF, 128)))
        peak[g] = wide
        inv[g] = 0.7071067811865476 / wide
    for n in range(4):
        cross(n).wait_recv()

    side = 1 - 2 * c

    def away(g, k):
        return lax.rem(y + g * (z - y) + 8 + side * k, 8)

    def coded(g, k):
        place = away(g, k)
        rows = pl.ds(pl.multiple_of(place * 16, 16), 16)
        mine = pl.ds(pl.multiple_of(c * HALF + place * 16, 16), 16)
        scale = jnp.concatenate([inv[g, rows, :]] * (GROUP // 128), axis=1)
        own = jnp.clip(rot[g, mine, :].astype(F32) * scale, -1.0, 1.0)
        return own + jnp.clip(other[g, rows, :].astype(F32) * scale, -1.0, 1.0)

    def first(g, n):
        hop = away(g, HOPS[n]) - away(g, 0)
        peer = (dp + hop * (2 * NZ - 14 * g), t)
        return pltpu.make_async_remote_copy(
            src_ref=code.at[g, n], dst_ref=land1.at[g, n],
            send_sem=send1.at[g, n], recv_sem=recv1.at[g, n],
            device_id=peer, device_id_type=MESH,
        )

    def send_first(g, carry):
        for n in (0, 1, 2):
            code[g, n] = coded(g, TARGETS[n]).astype(BF16)
            first(g, n).start()
        return carry

    def send_direct(g, carry):
        for n in (3, 4):
            code[g, n] = coded(g, TARGETS[n]).astype(BF16)
            first(g, n).start()
        return carry

    def relay(g, carry):
        for n, parts in ((5, (2,)), (6, (1, 0))):
            value = coded(g, TARGETS[n])
            for part_n in parts:
                first(g, part_n).wait_recv()
                value = value + land1[g, part_n].astype(F32)
            code[g, n] = value.astype(BF16)
            first(g, n).start()
        return carry

    def keep(g, carry):
        acc[g] = coded(g, 0)
        return carry

    for step in (send_first, send_direct, relay, keep):
        lax.fori_loop(0, 2, step, 0)

    def second(g, k):
        peer = device(y, shift(z, k, NZ), c) if g == 0 else device(shift(y, k, NY), z, c)
        return pltpu.make_async_remote_copy(
            src_ref=pack.at[g, shift((z, y)[g], k, 8)], dst_ref=land2.at[g, k],
            send_sem=send2.at[g, k], recv_sem=recv2.at[g, k],
            device_id=peer, device_id_type=MESH,
        )

    for n in (3, 4, 5, 6):
        for g in range(2):
            first(g, n).wait_recv()
            acc[g] = acc[g] + land1[g, n].astype(F32)
    for g in range(2):
        for block in range(16):
            w[g, block * 16:(block + 1) * 16, :] = acc[g, :, block * 128:(block + 1) * 128]
        for place in range(8):
            pack[g, place] = jnp.concatenate(
                [w[g, pl.ds(place * 2 + i, 16, stride=16), :] for i in range(2)], axis=0
            ).astype(BF16)
        for k in FAR_FIRST:
            second(g, k).start()

    for g in range(2):
        total = pack[g, (z, y)[g]].astype(F32)
        for k in FAR_FIRST:
            second(g, k).wait_recv()
            total = total + land2[g, k].astype(F32)
        for i in range(2):
            row = (y, z)[g] * 16 + (z, y)[g] * 2 + i
            value = total[i * 16:(i + 1) * 16]
            at = i * 32 + g * 16
            tot_ref[at:at + 16, :] = value
            dec_ref[at:at + 16, :] = value * (2.0 * peak[g, pl.ds(row, 1), :])

    for k in range(1, NT):
        tokens(k).wait_send()
    q1_all.wait_send()
    q2_all.wait_send()
    for g in range(2):
        for n in range(2):
            cross(2 * g + n).wait_send()
        for n in range(7):
            first(g, n).wait_send()
        for k in FAR_FIRST:
            second(g, k).wait_send()


def local(tokens_in, grad_hidden):
    dma = pltpu.SemaphoreType.DMA
    decoded, total = pl.pallas_call(
        kernel,
        out_shape=[jax.ShapeDtypeStruct((64, 128), F32)] * 2,
        in_specs=[
            pl.BlockSpec(memory_space=pltpu.VMEM),
            pl.BlockSpec(memory_space=pl.ANY),
        ],
        out_specs=[pl.BlockSpec(memory_space=pltpu.VMEM)] * 2,
        scratch_shapes=[
            pltpu.VMEM((SLOT, ROWS), F32),
            pltpu.VMEM((256, 256), BF16),
            pltpu.VMEM((NT, SLOT, ROWS), BF16),
            pltpu.VMEM((DEPTH, HID), BF16),
            pltpu.VMEM((2, ROWS, SLOT), BF16),
            pltpu.VMEM((ROWS, HID), F32),
            pltpu.VMEM((2, ROWS, GROUP), BF16),
            pltpu.VMEM((2, HALF, GROUP), BF16),
            pltpu.VMEM((2, ROWS, 128), F32),
            pltpu.VMEM((2, 2, 128), F32),
            pltpu.VMEM((2, 128), F32),
            pltpu.VMEM((16, 2, 128), F32),
            pltpu.VMEM((8, 2, 128), F32),
            pltpu.VMEM((2, HALF, 128), F32),
            pltpu.VMEM((2, HALF, 128), F32),
            pltpu.VMEM((2, 7, 16, GROUP), BF16),
            pltpu.VMEM((2, 7, 16, GROUP), BF16),
            pltpu.VMEM((2, 16, GROUP), F32),
            pltpu.VMEM((2, 256, 128), F32),
            pltpu.VMEM((2, 8, 32, 128), BF16),
            pltpu.VMEM((2, 8, 32, 128), BF16),
            dma, dma((NT,)), dma((NT,)), dma, dma, dma, dma, dma((4,)), dma((4,)),
            dma((2, 7)), dma((2, 7)), dma((2, 8)), dma((2, 8)),
        ],
        compiler_params=pltpu.CompilerParams(
            collective_id=0, has_side_effects=True, vmem_limit_bytes=53 * 1024 * 1024
        ),
        cost_estimate=pl.CostEstimate(
            flops=2 * DEPTH * ROWS * HID, bytes_accessed=2 * DEPTH * HID, transcendentals=0
        ),
    )(tokens_in, grad_hidden)
    return decoded.reshape(2, HID), total.reshape(2, HID)


def solution(mesh):
    placed = (P(("dp", "tensor"), None), P("dp", "tensor"))
    return jax.shard_map(
        local,
        mesh=mesh,
        in_specs=placed,
        out_specs=(P("dp", "tensor"), P("dp", "tensor")),
        check_vma=False,
    )
```

```python
import jax
import jax.numpy as jnp
from jax import lax
from jax.experimental import pallas as pl
from jax.experimental.pallas import tpu as pltpu
from jax.sharding import PartitionSpec as P

NY = 8
NZ = 8
NT = 4
TOKENS = 148
STEP = 144
SLOT = 160
DEPTH = 592
ROWS = 256
HALF = 128
HID = 4096
GROUP = 2048
EPS = 1e-06
F32 = jnp.float32
BF16 = jnp.bfloat16
MESH = pl.DeviceIdType.MESH
FAR_FIRST = (4, 3, 5, 2, 6, 1, 7)
RAW_TARGETS = (-4, -3, 3)
RAW_HOPS = (-2, -1, 1)
SUM_HOPS = (-2, 2, -1, 1)
RAW_PARTS = ((0, 1), (2,), (), ())


def row_order(group):
    new = lax.broadcasted_iota(jnp.int32, (ROWS, ROWS), 0)
    old = lax.broadcasted_iota(jnp.int32, (ROWS, ROWS), 1)
    core, first, second, i = new >> 7, (new >> 4) & 7, (new >> 1) & 7, new & 1
    y, z = (first, second) if group == 0 else (second, first)
    return jnp.where(old == 32 * y + 4 * z + 2 * core + i, 1.0, 0.0).astype(BF16)


def hadamard_pair():
    row = lax.broadcasted_iota(jnp.int32, (256, 256), 0)
    column = lax.broadcasted_iota(jnp.int32, (256, 256), 1)
    both = row & column & 127
    both = both ^ (both >> 4)
    both = both ^ (both >> 2)
    both = both ^ (both >> 1)
    sign = jnp.where((both & 1) == 0, 0.0625, -0.0625)
    return jnp.where((row >> 7) == (column >> 7), sign, 0.0).astype(BF16)


def kernel(
    tok_ref, grad_ref, dec_ref, tot_ref,
    tok, shifted, order, table, slots, gbuf, turned, part, rot, other, squares,
    qall, qfirst, q1, q2, inv, land0, code, land1, acc, w, pack, land2,
    far, gsem, toksem, tsend, trecv, q1send, q1recv, q2send, q2recv, xsend, xrecv, send0, recv0,
    send1, recv1, send2, recv2,
):
    dp = lax.axis_index("dp")
    t = lax.axis_index("tensor")
    c = lax.rem(dp, 2)
    z = lax.rem(lax.div(dp, 2), NZ)
    y = lax.div(dp, 2 * NZ)
    oc = 1 - c

    def device(yy, zz, cc):
        return (yy * (2 * NZ) + zz * 2 + cc, t)

    def shift(value, k, n):
        return lax.rem(value + k, n)

    barrier = pltpu.get_barrier_semaphore()
    peers_t = [(dp, shift(t, k, NT)) for k in range(1, NT)]
    peers_1 = [
        (kz * 2 + kc, shift(c, kc, 2), device(y, shift(z, kz, NZ), shift(c, kc, 2)))
        for kz in range(NZ)
        for kc in range(2)
        if kz + kc > 0
    ]
    peers_y = [device(shift(y, k, NY), z, c) for k in range(1, NY)]

    def along(g, k, core):
        place = lax.rem(y + g * (z - y) + 8 + (1 - 2 * core) * k, 8)
        return place, (dp + (place - y - g * (z - y)) * (2 * NZ - 14 * g) + core - c, t)

    near = list(peers_t) + [(dp + oc - c, t)]
    for g in range(2):
        for k in (1, -1, 2, -2):
            near += [along(g, k, c)[1], along(g, k, oc)[1]]
    for peer in near:
        pl.semaphore_signal(barrier, inc=1, device_id=peer, device_id_type=MESH)
    tok_copy = pltpu.make_async_copy(tok_ref, tok, toksem)
    tok_copy.start()
    grad_copy = pltpu.make_async_copy(grad_ref, gbuf, gsem)
    grad_copy.start()
    shifted[...] = jnp.zeros((SLOT, ROWS), F32)
    tok_copy.wait()
    shifted[0:TOKENS, :] = tok[...].astype(F32)
    slots[0] = pltpu.roll(shifted[...], 4 * t, 0).astype(BF16)
    pl.semaphore_wait(barrier, len(near))

    def tokens(k):
        return pltpu.make_async_remote_copy(
            src_ref=slots.at[0], dst_ref=slots.at[k],
            send_sem=tsend.at[k], recv_sem=trecv.at[k],
            device_id=(dp, shift(t, k, NT)), device_id_type=MESH,
        )

    for k in (1, 3, 2):
        tokens(k).start()
    for g in range(2):
        for k in (2, -2):
            pl.semaphore_signal(
                far, inc=1, device_id=along(g, k, c)[1], device_id_type=MESH
            )
    for g in range(2):
        order[g] = row_order(g)
    table[...] = hadamard_pair()
    squares[...] = jnp.zeros_like(squares)
    for k in (0, 1, 3, 2):
        source = shift(t, NT - k, NT)
        if k > 0:
            tokens(k).wait_recv()
        features = slots[k]
        for g in range(2):
            turned[g] = lax.dot_general(
                order[g], features, (((1,), (1,)), ((), ())), preferred_element_type=F32
            ).astype(BF16)
        if k == 0:
            grad_copy.wait()
        depth = pl.ds(pl.multiple_of(source * STEP, 16), SLOT)

        def columns(n, carry):
            g = lax.div(n, 2)
            left = turned[g]
            for tile in range(4):
                at = pl.ds(pl.multiple_of(n * 1024 + tile * 256, 256), 256)
                value = jnp.dot(left, gbuf[depth, at], preferred_element_type=F32)
                if k > 0:
                    value = part[:, at] + value
                part[:, at] = value
                if k == 2:
                    both = value * value
                    squares[g] = squares[g] + (both[:, :128] + both[:, 128:])
            return carry

        lax.fori_loop(0, 4, columns, 0)
    ones = jnp.ones((8, 128), F32)
    for g in range(2):
        q = lax.dot_general(
            ones, squares[g], (((1,), (1,)), ((), ())),
            preferred_element_type=F32, precision=lax.Precision.HIGHEST,
        )
        for half in range(2):
            qall[half, g:g + 1, :] = q[0:1, half * HALF:(half + 1) * HALF]

    pl.semaphore_wait(far, 4)

    for slot, core, peer in peers_1:
        pltpu.make_async_remote_copy(
            src_ref=qall.at[core], dst_ref=q1.at[slot],
            send_sem=q1send, recv_sem=q1recv, device_id=peer, device_id_type=MESH,
        ).start()

    def rotate(half, n):
        g, j = lax.div(n, 2), lax.rem(n, 2)
        rows = pl.ds(pl.multiple_of(half * HALF, HALF), HALF)
        value = jnp.concatenate(
            [
                part[rows, pl.ds(pl.multiple_of(n * 1024 + m * 256, 256), 256)]
                for m in range(4)
            ],
            axis=0,
        )
        high = value.astype(BF16)
        low = (value - high.astype(F32)).astype(BF16)
        result = (
            jnp.dot(high, table[...], preferred_element_type=F32)
            + jnp.dot(low, table[...], preferred_element_type=F32)
        ).astype(BF16)
        for m in range(4):
            at = pl.ds(pl.multiple_of(j * 1024 + m * 256, 256), 256)
            rot[g, rows, at] = result[m * HALF:(m + 1) * HALF]

    def cross(n):
        g, at = lax.div(n, 2), pl.ds(pl.multiple_of(lax.rem(n, 2) * 1024, 1024), 1024)
        return pltpu.make_async_remote_copy(
            src_ref=rot.at[g, pl.ds(pl.multiple_of(oc * HALF, HALF), HALF), at],
            dst_ref=other.at[g, :, at],
            send_sem=xsend.at[n], recv_sem=xrecv.at[n],
            device_id=device(y, z, oc), device_id_type=MESH,
        )

    def raw(g, other_core, j):
        core = shift(c, other_core, 2)
        place = along(g, RAW_TARGETS[j], core)[0]
        rows = pl.ds(pl.multiple_of(core * HALF + place * 16, 16), 16)
        n = other_core * 3 + j
        return pltpu.make_async_remote_copy(
            src_ref=rot.at[g, rows, :], dst_ref=land0.at[g, n],
            send_sem=send0.at[g, n], recv_sem=recv0.at[g, n],
            device_id=along(g, RAW_HOPS[j], core)[1], device_id_type=MESH,
        )

    def rotate_theirs(g, carry):
        for j in range(2):
            rotate(oc, 2 * g + j)
            cross(2 * g + j).start()
        for j in range(3):
            raw(g, 1, j).start()
        return carry

    def rotate_mine(g, carry):
        for j in range(2):
            rotate(c, 2 * g + j)
        for j in range(3):
            raw(g, 0, j).start()
        return carry

    lax.fori_loop(0, 2, rotate_theirs, 0)

    q1_all = pltpu.make_async_remote_copy(
        src_ref=q1.at[pl.ds(1, 15)], dst_ref=q1.at[pl.ds(1, 15)],
        send_sem=q1send, recv_sem=q1recv, device_id=device(y, z, oc), device_id_type=MESH,
    )
    q1_all.wait_recv()
    best = qall[c]
    for slot in range(1, 16):
        best = jnp.maximum(best, q1[slot])
    qfirst[...] = best
    for k in range(1, NY):
        pltpu.make_async_remote_copy(
            src_ref=qfirst, dst_ref=q2.at[k],
            send_sem=q2send, recv_sem=q2recv, device_id=peers_y[k - 1], device_id_type=MESH,
        ).start()
    lax.fori_loop(0, 2, rotate_mine, 0)
    q2_all = pltpu.make_async_remote_copy(
        src_ref=q2.at[pl.ds(1, 7)], dst_ref=q2.at[pl.ds(1, 7)],
        send_sem=q2send, recv_sem=q2recv, device_id=peers_y[0], device_id_type=MESH,
    )
    q2_all.wait_recv()
    best = qfirst[...]
    for k in range(1, NY):
        best = jnp.maximum(best, q2[k])
    best = 0.7071067811865476 / jnp.sqrt(best / float(GROUP) + EPS)
    for g in range(2):
        inv[g] = jnp.transpose(jnp.broadcast_to(best[g:g + 1, :], (HALF, 128)))
    for n in range(4):
        cross(n).wait_recv()

    def coded(g, k, parts):
        place = along(g, k, c)[0]
        rows = pl.ds(pl.multiple_of(place * 16, 16), 16)
        mine = pl.ds(pl.multiple_of(c * HALF + place * 16, 16), 16)
        scale = jnp.concatenate([inv[g, rows, :]] * (GROUP // 128), axis=1)
        value = jnp.clip(rot[g, mine, :].astype(F32) * scale, -1.0, 1.0)
        value = value + jnp.clip(other[g, rows, :].astype(F32) * scale, -1.0, 1.0)
        for j in parts:
            for n in (j, 3 + j):
                value = value + jnp.clip(land0[g, n].astype(F32) * scale, -1.0, 1.0)
        return value

    def first(g, n):
        return pltpu.make_async_remote_copy(
            src_ref=code.at[g, n], dst_ref=land1.at[g, n],
            send_sem=send1.at[g, n], recv_sem=recv1.at[g, n],
            device_id=along(g, SUM_HOPS[n], c)[1], device_id_type=MESH,
        )

    for n in range(4):
        def send_sum(g, carry, n=n):
            for j in RAW_PARTS[n]:
                for other_core in range(2):
                    raw(g, other_core, j).wait_recv()
            code[g, n] = coded(g, SUM_HOPS[n], RAW_PARTS[n]).astype(BF16)
            first(g, n).start()
            return carry

        lax.fori_loop(0, 2, send_sum, 0)

    def keep(g, carry):
        acc[g] = coded(g, 0, ())
        return carry

    lax.fori_loop(0, 2, keep, 0)

    def second(g, k):
        peer = device(y, shift(z, k, NZ), c) if g == 0 else device(shift(y, k, NY), z, c)
        return pltpu.make_async_remote_copy(
            src_ref=pack.at[g, shift((z, y)[g], k, 8)], dst_ref=land2.at[g, k],
            send_sem=send2.at[g, k], recv_sem=recv2.at[g, k],
            device_id=peer, device_id_type=MESH,
        )

    for g in range(2):
        value = acc[g]
        for n in (2, 3, 1, 0):
            first(g, n).wait_recv()
            value = value + land1[g, n].astype(F32)
        acc[g] = value
        for block in range(16):
            w[g, block * 16:(block + 1) * 16, :] = acc[g, :, block * 128:(block + 1) * 128]
        for place in range(8):
            pack[g, place] = jnp.concatenate(
                [w[g, pl.ds(place * 2 + i, 16, stride=16), :] for i in range(2)], axis=0
            ).astype(BF16)
        for k in FAR_FIRST:
            second(g, k).start()

    for g in range(2):
        total = pack[g, (z, y)[g]].astype(F32)
        for k in FAR_FIRST:
            second(g, k).wait_recv()
            total = total + land2[g, k].astype(F32)
        for i in range(2):
            row = (y, z)[g] * 16 + (z, y)[g] * 2 + i
            value = total[i * 16:(i + 1) * 16]
            at = g * 16
            scale = 1.4142135623730951 / inv[g, pl.ds(row, 1), :]
            tot_ref[at:at + 16, i, :] = value
            dec_ref[at:at + 16, i, :] = value * scale

    for k in range(1, NT):
        tokens(k).wait_send()
    q1_all.wait_send()
    q2_all.wait_send()
    for g in range(2):
        for n in range(2):
            cross(2 * g + n).wait_send()
        for j in range(3):
            raw(g, 0, j).wait_send()
            raw(g, 1, j).wait_send()
        for n in range(4):
            first(g, n).wait_send()
        for k in FAR_FIRST:
            second(g, k).wait_send()


def local(tokens_in, grad_hidden):
    dma = pltpu.SemaphoreType.DMA
    decoded, total = pl.pallas_call(
        kernel,
        out_shape=[jax.ShapeDtypeStruct((32, 2, 128), F32)] * 2,
        in_specs=[pl.BlockSpec(memory_space=pl.ANY)] * 2,
        out_specs=[pl.BlockSpec(memory_space=pltpu.VMEM)] * 2,
        scratch_shapes=[
            pltpu.VMEM((TOKENS, ROWS), BF16),
            pltpu.VMEM((SLOT, ROWS), F32),
            pltpu.VMEM((2, 256, 256), BF16),
            pltpu.VMEM((256, 256), BF16),
            pltpu.VMEM((NT, SLOT, ROWS), BF16),
            pltpu.VMEM((DEPTH, HID), BF16),
            pltpu.VMEM((2, ROWS, SLOT), BF16),
            pltpu.VMEM((ROWS, HID), F32),
            pltpu.VMEM((2, ROWS, GROUP), BF16),
            pltpu.VMEM((2, HALF, GROUP), BF16),
            pltpu.VMEM((2, ROWS, 128), F32),
            pltpu.VMEM((2, 2, 128), F32),
            pltpu.VMEM((2, 128), F32),
            pltpu.VMEM((16, 2, 128), F32),
            pltpu.VMEM((8, 2, 128), F32),
            pltpu.VMEM((2, HALF, 128), F32),
            pltpu.VMEM((2, 6, 16, GROUP), BF16),
            pltpu.VMEM((2, 4, 16, GROUP), BF16),
            pltpu.VMEM((2, 4, 16, GROUP), BF16),
            pltpu.VMEM((2, 16, GROUP), F32),
            pltpu.VMEM((2, 256, 128), F32),
            pltpu.VMEM((2, 8, 32, 128), BF16),
            pltpu.VMEM((2, 8, 32, 128), BF16),
            pltpu.SemaphoreType.REGULAR, dma, dma, dma((NT,)), dma((NT,)), dma, dma, dma, dma, dma((4,)), dma((4,)),
            dma((2, 6)), dma((2, 6)), dma((2, 4)), dma((2, 4)), dma((2, 8)), dma((2, 8)),
        ],
        compiler_params=pltpu.CompilerParams(
            collective_id=0, has_side_effects=True, vmem_limit_bytes=int(53.85 * 1024 * 1024)
        ),
        cost_estimate=pl.CostEstimate(
            flops=2 * DEPTH * ROWS * HID, bytes_accessed=2 * DEPTH * HID, transcendentals=0
        ),
    )(tokens_in, grad_hidden)
    return tuple(
        jnp.transpose(value, (1, 0, 2)).reshape(2, HID) for value in (decoded, total)
    )


def solution(mesh):
    placed = (P(("dp", "tensor"), None), P("dp", "tensor"))
    return jax.shard_map(
        local,
        mesh=mesh,
        in_specs=placed,
        out_specs=(P("dp", "tensor"), P("dp", "tensor")),
        check_vma=False,
    )
```

```python
import jax
import jax.numpy as jnp
from jax import lax
from jax.experimental import pallas as pl
from jax.experimental.pallas import tpu as pltpu
from jax.sharding import PartitionSpec as P

NY = 8
NZ = 8
NT = 4
TOKENS = 148
STEP = 144
SLOT = 160
DEPTH = 592
ROWS = 256
HALF = 128
HID = 4096
GROUP = 2048
EPS = 1e-06
F32 = jnp.float32
BF16 = jnp.bfloat16
MESH = pl.DeviceIdType.MESH
FAR_FIRST = (4, 3, 5, 2, 6, 1, 7)
RAW_TARGETS = (-4, -3, 3)
RAW_HOPS = (-2, -1, 1)
SUM_HOPS = (-2, 2, -1, 1)
RAW_PARTS = ((0, 1), (2,), (), ())


def row_order(group):
    new = lax.broadcasted_iota(jnp.int32, (ROWS, ROWS), 0)
    old = lax.broadcasted_iota(jnp.int32, (ROWS, ROWS), 1)
    core, first, second, i = new >> 7, (new >> 4) & 7, (new >> 1) & 7, new & 1
    y, z = (first, second) if group == 0 else (second, first)
    return jnp.where(old == 32 * y + 4 * z + 2 * core + i, 1.0, 0.0).astype(BF16)


def hadamard_pair():
    row = lax.broadcasted_iota(jnp.int32, (256, 256), 0)
    column = lax.broadcasted_iota(jnp.int32, (256, 256), 1)
    both = row & column & 127
    both = both ^ (both >> 4)
    both = both ^ (both >> 2)
    both = both ^ (both >> 1)
    sign = jnp.where((both & 1) == 0, 0.0625, -0.0625)
    return jnp.where((row >> 7) == (column >> 7), sign, 0.0).astype(BF16)


def kernel(
    tok_ref, grad_ref, out_ref,
    tok, shifted, order, table, slots, gbuf, turned, part, rot, other, squares,
    qall, qfirst, q1, q2, inv, land0, code, land1, acc, w, pack, land2,
    far, gsem, toksem, tsend, trecv, q1send, q1recv, q2send, q2recv, xsend, xrecv, send0, recv0,
    send1, recv1, send2, recv2,
):
    dp = lax.axis_index("dp")
    t = lax.axis_index("tensor")
    c = lax.rem(dp, 2)
    z = lax.rem(lax.div(dp, 2), NZ)
    y = lax.div(dp, 2 * NZ)
    oc = 1 - c

    def device(yy, zz, cc):
        return (yy * (2 * NZ) + zz * 2 + cc, t)

    def shift(value, k, n):
        return lax.rem(value + k, n)

    barrier = pltpu.get_barrier_semaphore()
    peers_t = [(dp, shift(t, k, NT)) for k in (1, 3)]
    peers_1 = [
        (kz * 2 + kc, shift(c, kc, 2), device(y, shift(z, kz, NZ), shift(c, kc, 2)))
        for kz in range(NZ)
        for kc in range(2)
        if kz + kc > 0
    ]
    peers_y = [device(shift(y, k, NY), z, c) for k in range(1, NY)]

    def along(g, k, core):
        place = lax.rem(y + g * (z - y) + 8 + (1 - 2 * core) * k, 8)
        return place, (dp + (place - y - g * (z - y)) * (2 * NZ - 14 * g) + core - c, t)

    near = list(peers_t) + [(dp + oc - c, t)]
    for g in range(2):
        for k in (1, -1, 2, -2):
            near += [along(g, k, c)[1], along(g, k, oc)[1]]
    for peer in near:
        pl.semaphore_signal(barrier, inc=1, device_id=peer, device_id_type=MESH)
    tok_copy = pltpu.make_async_copy(tok_ref, tok, toksem)
    tok_copy.start()
    grad_copy = pltpu.make_async_copy(grad_ref, gbuf, gsem)
    grad_copy.start()
    shifted[...] = jnp.zeros((SLOT, ROWS), F32)
    tok_copy.wait()
    shifted[0:TOKENS, :] = tok[...].astype(F32)
    slots[0] = pltpu.roll(shifted[...], 4 * t, 0).astype(BF16)
    pl.semaphore_wait(barrier, len(near))

    def tokens(k):
        return pltpu.make_async_remote_copy(
            src_ref=slots.at[0], dst_ref=slots.at[k],
            send_sem=tsend.at[k], recv_sem=trecv.at[k],
            device_id=(dp, shift(t, k, NT)), device_id_type=MESH,
        )

    def pass_on(k):
        rows = pl.ds(0 if k == 1 else SLOT // 2, SLOT // 2)
        return pltpu.make_async_remote_copy(
            src_ref=slots.at[k, rows], dst_ref=slots.at[2, rows],
            send_sem=tsend.at[k - 1], recv_sem=trecv.at[k - 1],
            device_id=(dp, shift(t, k, NT)), device_id_type=MESH,
        )

    for k in (1, 3):
        tokens(k).start()
    for g in range(2):
        for k in (2, -2):
            pl.semaphore_signal(
                far, inc=1, device_id=along(g, k, c)[1], device_id_type=MESH
            )
    for g in range(2):
        order[g] = row_order(g)
    table[...] = hadamard_pair()
    squares[...] = jnp.zeros_like(squares)
    for k in (0, 1, 3, 2):
        source = shift(t, NT - k, NT)
        if k == 1:
            for n in (1, 3):
                tokens(n).wait_recv()
                pass_on(n).start()
        if k == 2:
            for n in (1, 3):
                pass_on(n).wait_recv()
        features = slots[k]
        for g in range(2):
            turned[g] = lax.dot_general(
                order[g], features, (((1,), (1,)), ((), ())), preferred_element_type=F32
            ).astype(BF16)
        if k == 0:
            grad_copy.wait()
        depth = pl.ds(pl.multiple_of(source * STEP, 16), SLOT)

        def columns(n, carry):
            g = lax.div(n, 2)
            left = turned[g]
            for tile in range(4):
                at = pl.ds(pl.multiple_of(n * 1024 + tile * 256, 256), 256)
                value = jnp.dot(left, gbuf[depth, at], preferred_element_type=F32)
                if k > 0:
                    value = part[:, at] + value
                part[:, at] = value
                if k == 2:
                    both = value * value
                    squares[g] = squares[g] + (both[:, :128] + both[:, 128:])
            return carry

        lax.fori_loop(0, 4, columns, 0)
    ones = jnp.ones((8, 128), F32)
    for g in range(2):
        q = lax.dot_general(
            ones, squares[g], (((1,), (1,)), ((), ())),
            preferred_element_type=F32, precision=lax.Precision.HIGHEST,
        )
        for half in range(2):
            qall[half, g:g + 1, :] = q[0:1, half * HALF:(half + 1) * HALF]

    pl.semaphore_wait(far, 4)

    for slot, core, peer in peers_1:
        pltpu.make_async_remote_copy(
            src_ref=qall.at[core], dst_ref=q1.at[slot],
            send_sem=q1send, recv_sem=q1recv, device_id=peer, device_id_type=MESH,
        ).start()

    def rotate(half, n):
        g, j = lax.div(n, 2), lax.rem(n, 2)
        rows = pl.ds(pl.multiple_of(half * HALF, HALF), HALF)
        value = jnp.concatenate(
            [
                part[rows, pl.ds(pl.multiple_of(n * 1024 + m * 256, 256), 256)]
                for m in range(4)
            ],
            axis=0,
        )
        high = value.astype(BF16)
        low = (value - high.astype(F32)).astype(BF16)
        result = (
            jnp.dot(high, table[...], preferred_element_type=F32)
            + jnp.dot(low, table[...], preferred_element_type=F32)
        ).astype(BF16)
        for m in range(4):
            at = pl.ds(pl.multiple_of(j * 1024 + m * 256, 256), 256)
            rot[g, rows, at] = result[m * HALF:(m + 1) * HALF]

    def cross(n):
        g, at = lax.div(n, 2), pl.ds(pl.multiple_of(lax.rem(n, 2) * 1024, 1024), 1024)
        return pltpu.make_async_remote_copy(
            src_ref=rot.at[g, pl.ds(pl.multiple_of(oc * HALF, HALF), HALF), at],
            dst_ref=other.at[g, :, at],
            send_sem=xsend.at[n], recv_sem=xrecv.at[n],
            device_id=device(y, z, oc), device_id_type=MESH,
        )

    def raw(g, other_core, j):
        core = shift(c, other_core, 2)
        place = along(g, RAW_TARGETS[j], core)[0]
        rows = pl.ds(pl.multiple_of(core * HALF + place * 16, 16), 16)
        n = other_core * 3 + j
        return pltpu.make_async_remote_copy(
            src_ref=rot.at[g, rows, :], dst_ref=land0.at[g, n],
            send_sem=send0.at[g, n], recv_sem=recv0.at[g, n],
            device_id=along(g, RAW_HOPS[j], core)[1], device_id_type=MESH,
        )

    def rotate_theirs(g, carry):
        for j in range(2):
            rotate(oc, 2 * g + j)
            cross(2 * g + j).start()
        for j in range(3):
            raw(g, 1, j).start()
        return carry

    def rotate_mine(g, carry):
        for j in range(2):
            rotate(c, 2 * g + j)
        for j in range(3):
            raw(g, 0, j).start()
        return carry

    lax.fori_loop(0, 2, rotate_theirs, 0)
    lax.fori_loop(0, 2, rotate_mine, 0)

    q1_all = pltpu.make_async_remote_copy(
        src_ref=q1.at[pl.ds(1, 15)], dst_ref=q1.at[pl.ds(1, 15)],
        send_sem=q1send, recv_sem=q1recv, device_id=device(y, z, oc), device_id_type=MESH,
    )
    q1_all.wait_recv()
    best = qall[c]
    for slot in range(1, 16):
        best = jnp.maximum(best, q1[slot])
    qfirst[...] = best
    for k in range(1, NY):
        pltpu.make_async_remote_copy(
            src_ref=qfirst, dst_ref=q2.at[k],
            send_sem=q2send, recv_sem=q2recv, device_id=peers_y[k - 1], device_id_type=MESH,
        ).start()
    q2_all = pltpu.make_async_remote_copy(
        src_ref=q2.at[pl.ds(1, 7)], dst_ref=q2.at[pl.ds(1, 7)],
        send_sem=q2send, recv_sem=q2recv, device_id=peers_y[0], device_id_type=MESH,
    )
    q2_all.wait_recv()
    best = qfirst[...]
    for k in range(1, NY):
        best = jnp.maximum(best, q2[k])
    best = 0.7071067811865476 / jnp.sqrt(best / float(GROUP) + EPS)
    for g in range(2):
        inv[g] = jnp.transpose(jnp.broadcast_to(best[g:g + 1, :], (HALF, 128)))
    for n in range(4):
        cross(n).wait_recv()

    def coded(g, k, parts):
        place = along(g, k, c)[0]
        rows = pl.ds(pl.multiple_of(place * 16, 16), 16)
        mine = pl.ds(pl.multiple_of(c * HALF + place * 16, 16), 16)
        scale = jnp.concatenate([inv[g, rows, :]] * (GROUP // 128), axis=1)
        value = jnp.clip(rot[g, mine, :].astype(F32) * scale, -1.0, 1.0)
        value = value + jnp.clip(other[g, rows, :].astype(F32) * scale, -1.0, 1.0)
        for j in parts:
            for n in (j, 3 + j):
                value = value + jnp.clip(land0[g, n].astype(F32) * scale, -1.0, 1.0)
        return value

    def first(g, n):
        return pltpu.make_async_remote_copy(
            src_ref=code.at[g, n], dst_ref=land1.at[g, n],
            send_sem=send1.at[g, n], recv_sem=recv1.at[g, n],
            device_id=along(g, SUM_HOPS[n], c)[1], device_id_type=MESH,
        )

    for n in range(4):
        def send_sum(g, carry, n=n):
            for j in RAW_PARTS[n]:
                for other_core in range(2):
                    raw(g, other_core, j).wait_recv()
            code[g, n] = coded(g, SUM_HOPS[n], RAW_PARTS[n]).astype(BF16)
            first(g, n).start()
            return carry

        lax.fori_loop(0, 2, send_sum, 0)

    def keep(g, carry):
        acc[g] = coded(g, 0, ())
        return carry

    lax.fori_loop(0, 2, keep, 0)

    def second(g, k):
        peer = device(y, shift(z, k, NZ), c) if g == 0 else device(shift(y, k, NY), z, c)
        return pltpu.make_async_remote_copy(
            src_ref=pack.at[g, shift((z, y)[g], k, 8)], dst_ref=land2.at[g, k],
            send_sem=send2.at[g, k], recv_sem=recv2.at[g, k],
            device_id=peer, device_id_type=MESH,
        )

    for g in range(2):
        value = acc[g]
        for n in (2, 3, 1, 0):
            first(g, n).wait_recv()
            value = value + land1[g, n].astype(F32)
        acc[g] = value
        for block in range(16):
            w[g, block * 16:(block + 1) * 16, :] = acc[g, :, block * 128:(block + 1) * 128]
        for place in range(8):
            pack[g, place] = jnp.concatenate(
                [w[g, pl.ds(place * 2 + i, 16, stride=16), :] for i in range(2)], axis=0
            ).astype(BF16)
        for k in FAR_FIRST:
            second(g, k).start()

    for g in range(2):
        total = pack[g, (z, y)[g]].astype(F32)
        for k in FAR_FIRST:
            second(g, k).wait_recv()
            total = total + land2[g, k].astype(F32)
        for i in range(2):
            row = (y, z)[g] * 16 + (z, y)[g] * 2 + i
            value = total[i * 16:(i + 1) * 16]
            at = g * 16
            scale = 1.4142135623730951 / inv[g, pl.ds(row, 1), :]
            out_ref[1, at:at + 16, i, :] = value
            out_ref[0, at:at + 16, i, :] = value * scale

    for k in (1, 3):
        tokens(k).wait_send()
        pass_on(k).wait_send()
    q1_all.wait_send()
    q2_all.wait_send()
    for g in range(2):
        for n in range(2):
            cross(2 * g + n).wait_send()
        for j in range(3):
            raw(g, 0, j).wait_send()
            raw(g, 1, j).wait_send()
        for n in range(4):
            first(g, n).wait_send()
        for k in FAR_FIRST:
            second(g, k).wait_send()


def local(tokens_in, grad_hidden):
    dma = pltpu.SemaphoreType.DMA
    result = pl.pallas_call(
        kernel,
        out_shape=jax.ShapeDtypeStruct((2, 32, 2, 128), F32),
        in_specs=[pl.BlockSpec(memory_space=pl.ANY)] * 2,
        out_specs=pl.BlockSpec(memory_space=pltpu.VMEM),
        scratch_shapes=[
            pltpu.VMEM((TOKENS, ROWS), BF16),
            pltpu.VMEM((SLOT, ROWS), F32),
            pltpu.VMEM((2, 256, 256), BF16),
            pltpu.VMEM((256, 256), BF16),
            pltpu.VMEM((NT, SLOT, ROWS), BF16),
            pltpu.VMEM((DEPTH, HID), BF16),
            pltpu.VMEM((2, ROWS, SLOT), BF16),
            pltpu.VMEM((ROWS, HID), F32),
            pltpu.VMEM((2, ROWS, GROUP), BF16),
            pltpu.VMEM((2, HALF, GROUP), BF16),
            pltpu.VMEM((2, ROWS, 128), F32),
            pltpu.VMEM((2, 2, 128), F32),
            pltpu.VMEM((2, 128), F32),
            pltpu.VMEM((16, 2, 128), F32),
            pltpu.VMEM((8, 2, 128), F32),
            pltpu.VMEM((2, HALF, 128), F32),
            pltpu.VMEM((2, 6, 16, GROUP), BF16),
            pltpu.VMEM((2, 4, 16, GROUP), BF16),
            pltpu.VMEM((2, 4, 16, GROUP), BF16),
            pltpu.VMEM((2, 16, GROUP), F32),
            pltpu.VMEM((2, 256, 128), F32),
            pltpu.VMEM((2, 8, 32, 128), BF16),
            pltpu.VMEM((2, 8, 32, 128), BF16),
            pltpu.SemaphoreType.REGULAR, dma, dma, dma((NT,)), dma((NT,)), dma, dma, dma, dma, dma((4,)), dma((4,)),
            dma((2, 6)), dma((2, 6)), dma((2, 4)), dma((2, 4)), dma((2, 8)), dma((2, 8)),
        ],
        compiler_params=pltpu.CompilerParams(
            collective_id=0, has_side_effects=True, vmem_limit_bytes=int(53.85 * 1024 * 1024)
        ),
        cost_estimate=pl.CostEstimate(
            flops=2 * DEPTH * ROWS * HID, bytes_accessed=2 * DEPTH * HID, transcendentals=0
        ),
    )(tokens_in, grad_hidden)
    result = jnp.transpose(result, (0, 2, 1, 3)).reshape(2, 2, HID)
    return result[0], result[1]


def solution(mesh):
    placed = (P(("dp", "tensor"), None), P("dp", "tensor"))
    return jax.shard_map(
        local,
        mesh=mesh,
        in_specs=placed,
        out_specs=(P("dp", "tensor"), P("dp", "tensor")),
        check_vma=False,
    )
```

```python
import jax
import jax.numpy as jnp
from jax import lax
from jax.experimental import pallas as pl
from jax.experimental.pallas import tpu as pltpu
from jax.sharding import PartitionSpec as P

NY = 8
NZ = 8
NT = 4
TOKENS = 148
STEP = 144
SLOT = 160
DEPTH = 592
ROWS = 256
HALF = 128
HID = 4096
GROUP = 2048
EPS = 1e-06
F32 = jnp.float32
BF16 = jnp.bfloat16
MESH = pl.DeviceIdType.MESH
FAR_FIRST = (4, 3, 5, 2, 6, 1, 7)
RAW_TARGETS = (-4, -3, 3, -1, 1)
RAW_HOPS = (-2, -1, 1, -1, 1)
SUM_HOPS = (-2, 2)
RAW_PARTS = ((0, 1), (2,))
OWN_PARTS = (3, 4)


def row_order(group):
    new = lax.broadcasted_iota(jnp.int32, (ROWS, ROWS), 0)
    old = lax.broadcasted_iota(jnp.int32, (ROWS, ROWS), 1)
    core, first, second, i = new >> 7, (new >> 4) & 7, (new >> 1) & 7, new & 1
    y, z = (first, second) if group == 0 else (second, first)
    return jnp.where(old == 32 * y + 4 * z + 2 * core + i, 1.0, 0.0).astype(BF16)


def hadamard_pair():
    row = lax.broadcasted_iota(jnp.int32, (256, 256), 0)
    column = lax.broadcasted_iota(jnp.int32, (256, 256), 1)
    both = row & column & 127
    both = both ^ (both >> 4)
    both = both ^ (both >> 2)
    both = both ^ (both >> 1)
    sign = jnp.where((both & 1) == 0, 0.0625, -0.0625)
    return jnp.where((row >> 7) == (column >> 7), sign, 0.0).astype(BF16)


def kernel(
    tok_ref, grad_ref, out_ref,
    tok, shifted, order, table, slots, gbuf, turned, part, rot, other, squares,
    qall, qfirst, q1, q2, inv, land0, code, land1, acc, w, pack, land2,
    far, gsem, toksem, tsend, trecv, q1send, q1recv, q2send, q2recv, xsend, xrecv, send0, recv0,
    send1, recv1, send2, recv2,
):
    dp = lax.axis_index("dp")
    t = lax.axis_index("tensor")
    c = lax.rem(dp, 2)
    z = lax.rem(lax.div(dp, 2), NZ)
    y = lax.div(dp, 2 * NZ)
    oc = 1 - c

    def device(yy, zz, cc):
        return (yy * (2 * NZ) + zz * 2 + cc, t)

    def shift(value, k, n):
        return lax.rem(value + k, n)

    barrier = pltpu.get_barrier_semaphore()
    peers_t = [(dp, shift(t, k, NT)) for k in (1, 3)]
    peers_1 = [
        (kz * 2 + kc, shift(c, kc, 2), device(y, shift(z, kz, NZ), shift(c, kc, 2)))
        for kz in FAR_FIRST + (0,)
        for kc in (1, 0)
        if kz + kc > 0
    ]
    peers_y = [device(shift(y, k, NY), z, c) for k in range(1, NY)]

    def along(g, k, core):
        place = lax.rem(y + g * (z - y) + 8 + (1 - 2 * core) * k, 8)
        return place, (dp + (place - y - g * (z - y)) * (2 * NZ - 14 * g) + core - c, t)

    near = list(peers_t) + [(dp + oc - c, t)]
    for g in range(2):
        for k in (1, -1, 2, -2):
            near += [along(g, k, c)[1], along(g, k, oc)[1]]
    for peer in near:
        pl.semaphore_signal(barrier, inc=1, device_id=peer, device_id_type=MESH)
    tok_copy = pltpu.make_async_copy(tok_ref, tok, toksem)
    tok_copy.start()
    grad_copy = pltpu.make_async_copy(grad_ref, gbuf, gsem)
    grad_copy.start()
    shifted[...] = jnp.zeros((SLOT, ROWS), F32)
    tok_copy.wait()
    shifted[0:TOKENS, :] = tok[...].astype(F32)
    slots[0] = pltpu.roll(shifted[...], 4 * t, 0).astype(BF16)
    pl.semaphore_wait(barrier, len(near))

    def tokens(k):
        return pltpu.make_async_remote_copy(
            src_ref=slots.at[0], dst_ref=slots.at[k],
            send_sem=tsend.at[k], recv_sem=trecv.at[k],
            device_id=(dp, shift(t, k, NT)), device_id_type=MESH,
        )

    def pass_on(k):
        rows = pl.ds(0 if k == 1 else SLOT // 2, SLOT // 2)
        return pltpu.make_async_remote_copy(
            src_ref=slots.at[k, rows], dst_ref=slots.at[2, rows],
            send_sem=tsend.at[k - 1], recv_sem=trecv.at[k - 1],
            device_id=(dp, shift(t, k, NT)), device_id_type=MESH,
        )

    for k in (1, 3):
        tokens(k).start()
    for g in range(2):
        for k in (2, -2):
            pl.semaphore_signal(
                far, inc=1, device_id=along(g, k, c)[1], device_id_type=MESH
            )
    for g in range(2):
        order[g] = row_order(g)
    table[...] = hadamard_pair()
    for step, ks in enumerate(((0,), (1, 3), (2,))):
        if step == 1:
            for k in ks:
                tokens(k).wait_recv()
                pass_on(k).start()
        if step == 2:
            for k in (1, 3):
                pass_on(k).wait_recv()
        for n, k in enumerate(ks):
            features = slots[k]
            for g in range(2):
                turned[n, g] = lax.dot_general(
                    order[g], features, (((1,), (1,)), ((), ())),
                    preferred_element_type=F32,
                ).astype(BF16)
        if step == 0:
            grad_copy.wait()
        depths = [
            pl.ds(pl.multiple_of(shift(t, NT - k, NT) * STEP, 16), SLOT) for k in ks
        ]

        def columns(m, carry):
            g = lax.div(m, 2)
            total = None
            for tile in range(4):
                at = pl.ds(pl.multiple_of(m * 1024 + tile * 256, 256), 256)
                value = part[:, at] if step > 0 else None
                for n, depth in enumerate(depths):
                    product = jnp.dot(
                        turned[n, g], gbuf[depth, at], preferred_element_type=F32
                    )
                    value = product if value is None else value + product
                part[:, at] = value
                if step == 2:
                    both = value * value
                    both = both[:, :128] + both[:, 128:]
                    total = both if total is None else total + both
            if step == 2:
                squares[m] = total
            return carry

        lax.fori_loop(0, 4, columns, 0)
    ones = jnp.ones((8, 128), F32)
    for g in range(2):
        q = lax.dot_general(
            ones, squares[2 * g] + squares[2 * g + 1], (((1,), (1,)), ((), ())),
            preferred_element_type=F32, precision=lax.Precision.HIGHEST,
        )
        for half in range(2):
            qall[half, g:g + 1, :] = q[0:1, half * HALF:(half + 1) * HALF]

    pl.semaphore_wait(far, 4)

    for slot, core, peer in peers_1:
        pltpu.make_async_remote_copy(
            src_ref=qall.at[core], dst_ref=q1.at[slot],
            send_sem=q1send, recv_sem=q1recv, device_id=peer, device_id_type=MESH,
        ).start()

    def rotate(half, n):
        g, j = lax.div(n, 2), lax.rem(n, 2)
        rows = pl.ds(pl.multiple_of(half * HALF, HALF), HALF)
        value = jnp.concatenate(
            [
                part[rows, pl.ds(pl.multiple_of(n * 1024 + m * 256, 256), 256)]
                for m in range(4)
            ],
            axis=0,
        )
        high = value.astype(BF16)
        low = (value - high.astype(F32)).astype(BF16)
        result = (
            jnp.dot(high, table[...], preferred_element_type=F32)
            + jnp.dot(low, table[...], preferred_element_type=F32)
        ).astype(BF16)
        for m in range(4):
            at = pl.ds(pl.multiple_of(j * 1024 + m * 256, 256), 256)
            rot[g, rows, at] = result[m * HALF:(m + 1) * HALF]

    def cross(n):
        g, at = lax.div(n, 2), pl.ds(pl.multiple_of(lax.rem(n, 2) * 1024, 1024), 1024)
        return pltpu.make_async_remote_copy(
            src_ref=rot.at[g, pl.ds(pl.multiple_of(oc * HALF, HALF), HALF), at],
            dst_ref=other.at[g, :, at],
            send_sem=xsend.at[n], recv_sem=xrecv.at[n],
            device_id=device(y, z, oc), device_id_type=MESH,
        )

    def raw(g, other_core, j):
        core = shift(c, other_core, 2)
        place = along(g, RAW_TARGETS[j], core)[0]
        rows = pl.ds(pl.multiple_of(core * HALF + place * 16, 16), 16)
        n = other_core * 5 + j
        return pltpu.make_async_remote_copy(
            src_ref=rot.at[g, rows, :], dst_ref=land0.at[g, n],
            send_sem=send0.at[g, n], recv_sem=recv0.at[g, n],
            device_id=along(g, RAW_HOPS[j], core)[1], device_id_type=MESH,
        )

    def rotate_theirs(g, carry):
        for j in range(2):
            rotate(oc, 2 * g + j)
            cross(2 * g + j).start()
        for j in range(5):
            raw(g, 1, j).start()
        return carry

    def rotate_mine(g, carry):
        for j in range(2):
            rotate(c, 2 * g + j)
        for j in range(5):
            raw(g, 0, j).start()
        return carry

    lax.fori_loop(0, 2, rotate_theirs, 0)
    lax.fori_loop(0, 2, rotate_mine, 0)

    q1_all = pltpu.make_async_remote_copy(
        src_ref=q1.at[pl.ds(1, 15)], dst_ref=q1.at[pl.ds(1, 15)],
        send_sem=q1send, recv_sem=q1recv, device_id=device(y, z, oc), device_id_type=MESH,
    )
    q1_all.wait_recv()
    best = qall[c]
    for slot in range(1, 16):
        best = jnp.maximum(best, q1[slot])
    qfirst[...] = best
    for k in FAR_FIRST:
        pltpu.make_async_remote_copy(
            src_ref=qfirst, dst_ref=q2.at[k],
            send_sem=q2send, recv_sem=q2recv, device_id=peers_y[k - 1], device_id_type=MESH,
        ).start()
    q2_all = pltpu.make_async_remote_copy(
        src_ref=q2.at[pl.ds(1, 7)], dst_ref=q2.at[pl.ds(1, 7)],
        send_sem=q2send, recv_sem=q2recv, device_id=peers_y[0], device_id_type=MESH,
    )
    q2_all.wait_recv()
    best = qfirst[...]
    for k in range(1, NY):
        best = jnp.maximum(best, q2[k])
    best = 0.7071067811865476 / jnp.sqrt(best / float(GROUP) + EPS)
    for g in range(2):
        inv[g] = jnp.transpose(jnp.broadcast_to(best[g:g + 1, :], (HALF, 128)))
    for n in range(4):
        cross(n).wait_recv()

    def coded(g, k, parts):
        place = along(g, k, c)[0]
        rows = pl.ds(pl.multiple_of(place * 16, 16), 16)
        mine = pl.ds(pl.multiple_of(c * HALF + place * 16, 16), 16)
        scale = jnp.concatenate([inv[g, rows, :]] * (GROUP // 128), axis=1)
        value = jnp.clip(rot[g, mine, :].astype(F32) * scale, -1.0, 1.0)
        value = value + jnp.clip(other[g, rows, :].astype(F32) * scale, -1.0, 1.0)
        for j in parts:
            for n in (j, 5 + j):
                value = value + jnp.clip(land0[g, n].astype(F32) * scale, -1.0, 1.0)
        return value

    def first(g, n):
        return pltpu.make_async_remote_copy(
            src_ref=code.at[g, n], dst_ref=land1.at[g, n],
            send_sem=send1.at[g, n], recv_sem=recv1.at[g, n],
            device_id=along(g, SUM_HOPS[n], c)[1], device_id_type=MESH,
        )

    def arrived(g, parts):
        for j in parts:
            for other_core in range(2):
                raw(g, other_core, j).wait_recv()

    for n in range(2):
        def send_sum(g, carry, n=n):
            arrived(g, RAW_PARTS[n])
            code[g, n] = coded(g, SUM_HOPS[n], RAW_PARTS[n]).astype(BF16)
            first(g, n).start()
            return carry

        lax.fori_loop(0, 2, send_sum, 0)

    def keep(g, carry):
        arrived(g, OWN_PARTS)
        acc[g] = coded(g, 0, OWN_PARTS)
        return carry

    lax.fori_loop(0, 2, keep, 0)

    def second(g, k):
        peer = device(y, shift(z, k, NZ), c) if g == 0 else device(shift(y, k, NY), z, c)
        return pltpu.make_async_remote_copy(
            src_ref=pack.at[g, shift((z, y)[g], k, 8)], dst_ref=land2.at[g, k],
            send_sem=send2.at[g, k], recv_sem=recv2.at[g, k],
            device_id=peer, device_id_type=MESH,
        )

    for g in range(2):
        value = acc[g]
        for n in (1, 0):
            first(g, n).wait_recv()
            value = value + land1[g, n].astype(F32)
        acc[g] = value
        for block in range(16):
            w[g, block * 16:(block + 1) * 16, :] = acc[g, :, block * 128:(block + 1) * 128]
        for place in range(8):
            pack[g, place] = jnp.concatenate(
                [w[g, pl.ds(place * 2 + i, 16, stride=16), :] for i in range(2)], axis=0
            ).astype(BF16)
        for k in FAR_FIRST:
            second(g, k).start()

    for g in range(2):
        total = pack[g, (z, y)[g]].astype(F32)
        for k in FAR_FIRST:
            second(g, k).wait_recv()
            total = total + land2[g, k].astype(F32)
        for i in range(2):
            row = (y, z)[g] * 16 + (z, y)[g] * 2 + i
            value = total[i * 16:(i + 1) * 16]
            at = g * 16
            scale = 1.4142135623730951 / inv[g, pl.ds(row, 1), :]
            out_ref[1, at:at + 16, i, :] = value
            out_ref[0, at:at + 16, i, :] = value * scale

    for k in (1, 3):
        tokens(k).wait_send()
        pass_on(k).wait_send()
    q1_all.wait_send()
    q2_all.wait_send()
    for g in range(2):
        for n in range(2):
            cross(2 * g + n).wait_send()
        for j in range(5):
            raw(g, 0, j).wait_send()
            raw(g, 1, j).wait_send()
        for n in range(2):
            first(g, n).wait_send()
        for k in FAR_FIRST:
            second(g, k).wait_send()


def local(tokens_in, grad_hidden):
    dma = pltpu.SemaphoreType.DMA
    result = pl.pallas_call(
        kernel,
        out_shape=jax.ShapeDtypeStruct((2, 32, 2, 128), F32),
        in_specs=[pl.BlockSpec(memory_space=pl.ANY)] * 2,
        out_specs=pl.BlockSpec(memory_space=pltpu.VMEM),
        scratch_shapes=[
            pltpu.VMEM((TOKENS, ROWS), BF16),
            pltpu.VMEM((SLOT, ROWS), F32),
            pltpu.VMEM((2, 256, 256), BF16),
            pltpu.VMEM((256, 256), BF16),
            pltpu.VMEM((NT, SLOT, ROWS), BF16),
            pltpu.VMEM((DEPTH, HID), BF16),
            pltpu.VMEM((2, 2, ROWS, SLOT), BF16),
            pltpu.VMEM((ROWS, HID), F32),
            pltpu.VMEM((2, ROWS, GROUP), BF16),
            pltpu.VMEM((2, HALF, GROUP), BF16),
            pltpu.VMEM((4, ROWS, 128), F32),
            pltpu.VMEM((2, 2, 128), F32),
            pltpu.VMEM((2, 128), F32),
            pltpu.VMEM((16, 2, 128), F32),
            pltpu.VMEM((8, 2, 128), F32),
            pltpu.VMEM((2, HALF, 128), F32),
            pltpu.VMEM((2, 10, 16, GROUP), BF16),
            pltpu.VMEM((2, 2, 16, GROUP), BF16),
            pltpu.VMEM((2, 2, 16, GROUP), BF16),
            pltpu.VMEM((2, 16, GROUP), F32),
            pltpu.VMEM((2, 256, 128), F32),
            pltpu.VMEM((2, 8, 32, 128), BF16),
            pltpu.VMEM((2, 8, 32, 128), BF16),
            pltpu.SemaphoreType.REGULAR, dma, dma, dma((NT,)), dma((NT,)), dma, dma, dma, dma, dma((4,)), dma((4,)),
            dma((2, 10)), dma((2, 10)), dma((2, 2)), dma((2, 2)), dma((2, 8)), dma((2, 8)),
        ],
        compiler_params=pltpu.CompilerParams(
            collective_id=0, has_side_effects=True, vmem_limit_bytes=int(53.85 * 1024 * 1024)
        ),
        cost_estimate=pl.CostEstimate(
            flops=2 * DEPTH * ROWS * HID, bytes_accessed=2 * DEPTH * HID, transcendentals=0
        ),
    )(tokens_in, grad_hidden)
    result = jnp.transpose(result, (0, 2, 1, 3)).reshape(2, 2, HID)
    return result[0], result[1]


def solution(mesh):
    placed = (P(("dp", "tensor"), None), P("dp", "tensor"))
    return jax.shard_map(
        local,
        mesh=mesh,
        in_specs=placed,
        out_specs=(P("dp", "tensor"), P("dp", "tensor")),
        check_vma=False,
    )
```

```python
import jax
import jax.numpy as jnp
from jax import lax
from jax.experimental import pallas as pl
from jax.experimental.pallas import tpu as pltpu
from jax.sharding import PartitionSpec as P

NY = 8
NZ = 8
NT = 4
TOKENS = 148
STEP = 144
SLOT = 160
DEPTH = 592
ROWS = 256
HALF = 128
HID = 4096
GROUP = 2048
EPS = 1e-06
F32 = jnp.float32
BF16 = jnp.bfloat16
MESH = pl.DeviceIdType.MESH
FAR_FIRST = (4, 3, 5, 2, 6, 1, 7)
RAW_TARGETS = (-4, -3, 3)
RAW_HOPS = (-2, -1, 1)
SUM_HOPS = (-2, 2, -1, 1)
RAW_PARTS = ((0, 1), (2,), (), ())


def row_order(group):
    new = lax.broadcasted_iota(jnp.int32, (ROWS, ROWS), 0)
    old = lax.broadcasted_iota(jnp.int32, (ROWS, ROWS), 1)
    core, first, second, i = new >> 7, (new >> 4) & 7, (new >> 1) & 7, new & 1
    y, z = (first, second) if group == 0 else (second, first)
    return jnp.where(old == 32 * y + 4 * z + 2 * core + i, 1.0, 0.0).astype(BF16)


def hadamard_pair():
    row = lax.broadcasted_iota(jnp.int32, (256, 256), 0)
    column = lax.broadcasted_iota(jnp.int32, (256, 256), 1)
    both = row & column & 127
    both = both ^ (both >> 4)
    both = both ^ (both >> 2)
    both = both ^ (both >> 1)
    sign = jnp.where((both & 1) == 0, 0.0625, -0.0625)
    return jnp.where((row >> 7) == (column >> 7), sign, 0.0).astype(BF16)


def kernel(
    tok_ref, grad_ref, out_ref,
    tok, shifted, order, table, slots, gbuf, turned, part, rot, other, squares,
    qall, qfirst, q1, q2, inv, ahead, land0, code, land1, acc, w, pack, land2,
    far, gsem, toksem, tsend, trecv, q1send, q1recv, q2send, q2recv, xsend, xrecv, send0, recv0,
    send1, recv1, send2, recv2,
):
    dp = lax.axis_index("dp")
    t = lax.axis_index("tensor")
    c = lax.rem(dp, 2)
    z = lax.rem(lax.div(dp, 2), NZ)
    y = lax.div(dp, 2 * NZ)
    oc = 1 - c

    def device(yy, zz, cc):
        return (yy * (2 * NZ) + zz * 2 + cc, t)

    def shift(value, k, n):
        return lax.rem(value + k, n)

    barrier = pltpu.get_barrier_semaphore()
    peers_t = [(dp, shift(t, k, NT)) for k in (1, 3)]
    peers_1 = [
        (kz * 2 + kc, shift(c, kc, 2), device(y, shift(z, kz, NZ), shift(c, kc, 2)))
        for kz in FAR_FIRST + (0,)
        for kc in (1, 0)
        if kz + kc > 0
    ]
    peers_y = [device(shift(y, k, NY), z, c) for k in range(1, NY)]

    def along(g, k, core):
        place = lax.rem(y + g * (z - y) + 8 + (1 - 2 * core) * k, 8)
        return place, (dp + (place - y - g * (z - y)) * (2 * NZ - 14 * g) + core - c, t)

    near = list(peers_t) + [(dp + oc - c, t)]
    for g in range(2):
        for k in (1, -1, 2, -2):
            near += [along(g, k, c)[1], along(g, k, oc)[1]]
    for peer in near:
        pl.semaphore_signal(barrier, inc=1, device_id=peer, device_id_type=MESH)
    tok_copy = pltpu.make_async_copy(tok_ref, tok, toksem)
    tok_copy.start()
    grad_copy = pltpu.make_async_copy(grad_ref, gbuf, gsem)
    grad_copy.start()
    shifted[...] = jnp.zeros((SLOT, ROWS), F32)
    tok_copy.wait()
    shifted[0:TOKENS, :] = tok[...].astype(F32)
    slots[0] = pltpu.roll(shifted[...], 4 * t, 0).astype(BF16)
    pl.semaphore_wait(barrier, len(near))

    def tokens(k):
        return pltpu.make_async_remote_copy(
            src_ref=slots.at[0], dst_ref=slots.at[k],
            send_sem=tsend.at[k], recv_sem=trecv.at[k],
            device_id=(dp, shift(t, k, NT)), device_id_type=MESH,
        )

    def pass_on(k):
        rows = pl.ds(0 if k == 1 else SLOT // 2, SLOT // 2)
        return pltpu.make_async_remote_copy(
            src_ref=slots.at[k, rows], dst_ref=slots.at[2, rows],
            send_sem=tsend.at[k - 1], recv_sem=trecv.at[k - 1],
            device_id=(dp, shift(t, k, NT)), device_id_type=MESH,
        )

    for k in (1, 3):
        tokens(k).start()
    for g in range(2):
        for k in (2, -2):
            pl.semaphore_signal(
                far, inc=1, device_id=along(g, k, c)[1], device_id_type=MESH
            )
    for g in range(2):
        order[g] = row_order(g)
    table[...] = hadamard_pair()
    for step, ks in enumerate(((0,), (1, 3), (2,))):
        if step == 1:
            for k in ks:
                tokens(k).wait_recv()
                pass_on(k).start()
        if step == 2:
            for k in (1, 3):
                pass_on(k).wait_recv()
        for n, k in enumerate(ks):
            features = slots[k]
            for g in range(2):
                turned[n, g] = lax.dot_general(
                    order[g], features, (((1,), (1,)), ((), ())),
                    preferred_element_type=F32,
                ).astype(BF16)
        if step == 0:
            grad_copy.wait()
        depths = [
            pl.ds(pl.multiple_of(shift(t, NT - k, NT) * STEP, 16), SLOT) for k in ks
        ]

        def columns(m, carry):
            g = lax.div(m, 2)
            total = None
            for tile in range(4):
                at = pl.ds(pl.multiple_of(m * 1024 + tile * 256, 256), 256)
                value = part[:, at] if step > 0 else None
                for n, depth in enumerate(depths):
                    product = jnp.dot(
                        turned[n, g], gbuf[depth, at], preferred_element_type=F32
                    )
                    value = product if value is None else value + product
                part[:, at] = value
                if step == 2:
                    both = value * value
                    both = both[:, :128] + both[:, 128:]
                    total = both if total is None else total + both
            if step == 2:
                squares[m] = total
            return carry

        lax.fori_loop(0, 4, columns, 0)
    ones = jnp.ones((8, 128), F32)
    for g in range(2):
        q = lax.dot_general(
            ones, squares[2 * g] + squares[2 * g + 1], (((1,), (1,)), ((), ())),
            preferred_element_type=F32, precision=lax.Precision.HIGHEST,
        )
        for half in range(2):
            qall[half, g:g + 1, :] = q[0:1, half * HALF:(half + 1) * HALF]

    pl.semaphore_wait(far, 4)

    for slot, core, peer in peers_1:
        pltpu.make_async_remote_copy(
            src_ref=qall.at[core], dst_ref=q1.at[slot],
            send_sem=q1send, recv_sem=q1recv, device_id=peer, device_id_type=MESH,
        ).start()

    def turn(value):
        high = value.astype(BF16)
        low = (value - high.astype(F32)).astype(BF16)
        return (
            jnp.dot(high, table[...], preferred_element_type=F32)
            + jnp.dot(low, table[...], preferred_element_type=F32)
        ).astype(BF16)

    def rotate(half, n):
        g, j = lax.div(n, 2), lax.rem(n, 2)
        rows = pl.ds(pl.multiple_of(half * HALF, HALF), HALF)
        value = jnp.concatenate(
            [
                part[rows, pl.ds(pl.multiple_of(n * 1024 + m * 256, 256), 256)]
                for m in range(4)
            ],
            axis=0,
        )
        result = turn(value)
        for m in range(4):
            at = pl.ds(pl.multiple_of(j * 1024 + m * 256, 256), 256)
            rot[g, rows, at] = result[m * HALF:(m + 1) * HALF]

    def cross(n):
        g, at = lax.div(n, 2), pl.ds(pl.multiple_of(lax.rem(n, 2) * 1024, 1024), 1024)
        return pltpu.make_async_remote_copy(
            src_ref=rot.at[g, pl.ds(pl.multiple_of(oc * HALF, HALF), HALF), at],
            dst_ref=other.at[g, :, at],
            send_sem=xsend.at[n], recv_sem=xrecv.at[n],
            device_id=device(y, z, oc), device_id_type=MESH,
        )

    def raw(g, other_core, j):
        core = shift(c, other_core, 2)
        n = other_core * 3 + j
        return pltpu.make_async_remote_copy(
            src_ref=ahead.at[g, n], dst_ref=land0.at[g, n],
            send_sem=send0.at[g, n], recv_sem=recv0.at[g, n],
            device_id=along(g, RAW_HOPS[j], core)[1], device_id_type=MESH,
        )

    def send_raw(js):
        chunks = [(j, g, n) for j in js for n in range(2) for g in range(2)]
        values = []
        for j, g, n in chunks:
            core = shift(c, n, 2)
            place = along(g, RAW_TARGETS[j], core)[0]
            rows = pl.ds(pl.multiple_of(core * HALF + place * 16, 16), 16)
            values += [
                part[rows, g * GROUP + m * 256:g * GROUP + (m + 1) * 256] for m in range(8)
            ]
        result = turn(jnp.concatenate(values, axis=0))
        for i, (j, g, n) in enumerate(chunks):
            for m in range(8):
                at = i * 128 + m * 16
                ahead[g, n * 3 + j, :, m * 256:(m + 1) * 256] = result[at:at + 16]
            raw(g, n, j).start()

    def rotate_theirs(g, carry):
        for j in range(2):
            rotate(oc, 2 * g + j)
            cross(2 * g + j).start()
        return carry

    def rotate_mine(g, carry):
        for j in range(2):
            rotate(c, 2 * g + j)
        return carry

    send_raw((0,))
    send_raw((1, 2))
    lax.fori_loop(0, 2, rotate_theirs, 0)

    q1_all = pltpu.make_async_remote_copy(
        src_ref=q1.at[pl.ds(1, 15)], dst_ref=q1.at[pl.ds(1, 15)],
        send_sem=q1send, recv_sem=q1recv, device_id=device(y, z, oc), device_id_type=MESH,
    )
    q1_all.wait_recv()
    best = qall[c]
    for slot in range(1, 16):
        best = jnp.maximum(best, q1[slot])
    qfirst[...] = best
    for k in FAR_FIRST:
        pltpu.make_async_remote_copy(
            src_ref=qfirst, dst_ref=q2.at[k],
            send_sem=q2send, recv_sem=q2recv, device_id=peers_y[k - 1], device_id_type=MESH,
        ).start()
    lax.fori_loop(0, 2, rotate_mine, 0)
    q2_all = pltpu.make_async_remote_copy(
        src_ref=q2.at[pl.ds(1, 7)], dst_ref=q2.at[pl.ds(1, 7)],
        send_sem=q2send, recv_sem=q2recv, device_id=peers_y[0], device_id_type=MESH,
    )
    q2_all.wait_recv()
    best = qfirst[...]
    for k in range(1, NY):
        best = jnp.maximum(best, q2[k])
    best = 0.7071067811865476 / jnp.sqrt(best / float(GROUP) + EPS)
    for g in range(2):
        inv[g] = jnp.transpose(jnp.broadcast_to(best[g:g + 1, :], (HALF, 128)))
    for n in range(4):
        cross(n).wait_recv()

    def coded(g, k, parts):
        place = along(g, k, c)[0]
        rows = pl.ds(pl.multiple_of(place * 16, 16), 16)
        mine = pl.ds(pl.multiple_of(c * HALF + place * 16, 16), 16)
        scale = jnp.concatenate([inv[g, rows, :]] * (GROUP // 128), axis=1)
        value = jnp.clip(rot[g, mine, :].astype(F32) * scale, -1.0, 1.0)
        value = value + jnp.clip(other[g, rows, :].astype(F32) * scale, -1.0, 1.0)
        for j in parts:
            for n in (j, 3 + j):
                value = value + jnp.clip(land0[g, n].astype(F32) * scale, -1.0, 1.0)
        return value

    def first(g, n):
        return pltpu.make_async_remote_copy(
            src_ref=code.at[g, n], dst_ref=land1.at[g, n],
            send_sem=send1.at[g, n], recv_sem=recv1.at[g, n],
            device_id=along(g, SUM_HOPS[n], c)[1], device_id_type=MESH,
        )

    def arrived(g, parts):
        for j in parts:
            for other_core in range(2):
                raw(g, other_core, j).wait_recv()

    for n in range(4):
        def send_sum(g, carry, n=n):
            arrived(g, RAW_PARTS[n])
            code[g, n] = coded(g, SUM_HOPS[n], RAW_PARTS[n]).astype(BF16)
            first(g, n).start()
            return carry

        lax.fori_loop(0, 2, send_sum, 0)

    def keep(g, carry):
        acc[g] = coded(g, 0, ())
        return carry

    lax.fori_loop(0, 2, keep, 0)

    def second(g, k):
        peer = device(y, shift(z, k, NZ), c) if g == 0 else device(shift(y, k, NY), z, c)
        return pltpu.make_async_remote_copy(
            src_ref=pack.at[g, shift((z, y)[g], k, 8)], dst_ref=land2.at[g, k],
            send_sem=send2.at[g, k], recv_sem=recv2.at[g, k],
            device_id=peer, device_id_type=MESH,
        )

    for g in range(2):
        value = acc[g]
        for n in (2, 3, 1, 0):
            first(g, n).wait_recv()
            value = value + land1[g, n].astype(F32)
        acc[g] = value
        for block in range(16):
            w[g, block * 16:(block + 1) * 16, :] = acc[g, :, block * 128:(block + 1) * 128]
        for place in range(8):
            pack[g, place] = jnp.concatenate(
                [w[g, pl.ds(place * 2 + i, 16, stride=16), :] for i in range(2)], axis=0
            ).astype(BF16)
        for k in FAR_FIRST:
            second(g, k).start()

    for g in range(2):
        total = pack[g, (z, y)[g]].astype(F32)
        for k in FAR_FIRST:
            second(g, k).wait_recv()
            total = total + land2[g, k].astype(F32)
        for i in range(2):
            row = (y, z)[g] * 16 + (z, y)[g] * 2 + i
            value = total[i * 16:(i + 1) * 16]
            at = g * 16
            scale = 1.4142135623730951 / inv[g, pl.ds(row, 1), :]
            out_ref[1, at:at + 16, i, :] = value
            out_ref[0, at:at + 16, i, :] = value * scale

    for k in (1, 3):
        tokens(k).wait_send()
        pass_on(k).wait_send()
    q1_all.wait_send()
    q2_all.wait_send()
    for g in range(2):
        for n in range(2):
            cross(2 * g + n).wait_send()
        for j in range(3):
            raw(g, 0, j).wait_send()
            raw(g, 1, j).wait_send()
        for n in range(4):
            first(g, n).wait_send()
        for k in FAR_FIRST:
            second(g, k).wait_send()


def local(tokens_in, grad_hidden):
    dma = pltpu.SemaphoreType.DMA
    result = pl.pallas_call(
        kernel,
        out_shape=jax.ShapeDtypeStruct((2, 32, 2, 128), F32),
        in_specs=[pl.BlockSpec(memory_space=pl.ANY)] * 2,
        out_specs=pl.BlockSpec(memory_space=pltpu.VMEM),
        scratch_shapes=[
            pltpu.VMEM((TOKENS, ROWS), BF16),
            pltpu.VMEM((SLOT, ROWS), F32),
            pltpu.VMEM((2, 256, 256), BF16),
            pltpu.VMEM((256, 256), BF16),
            pltpu.VMEM((NT, SLOT, ROWS), BF16),
            pltpu.VMEM((DEPTH, HID), BF16),
            pltpu.VMEM((2, 2, ROWS, SLOT), BF16),
            pltpu.VMEM((ROWS, HID), F32),
            pltpu.VMEM((2, ROWS, GROUP), BF16),
            pltpu.VMEM((2, HALF, GROUP), BF16),
            pltpu.VMEM((4, ROWS, 128), F32),
            pltpu.VMEM((2, 2, 128), F32),
            pltpu.VMEM((2, 128), F32),
            pltpu.VMEM((16, 2, 128), F32),
            pltpu.VMEM((8, 2, 128), F32),
            pltpu.VMEM((2, HALF, 128), F32),
            pltpu.VMEM((2, 6, 16, GROUP), BF16),
            pltpu.VMEM((2, 6, 16, GROUP), BF16),
            pltpu.VMEM((2, 4, 16, GROUP), BF16),
            pltpu.VMEM((2, 4, 16, GROUP), BF16),
            pltpu.VMEM((2, 16, GROUP), F32),
            pltpu.VMEM((2, 256, 128), F32),
            pltpu.VMEM((2, 8, 32, 128), BF16),
            pltpu.VMEM((2, 8, 32, 128), BF16),
            pltpu.SemaphoreType.REGULAR, dma, dma, dma((NT,)), dma((NT,)), dma, dma, dma, dma, dma((4,)), dma((4,)),
            dma((2, 6)), dma((2, 6)), dma((2, 4)), dma((2, 4)), dma((2, 8)), dma((2, 8)),
        ],
        compiler_params=pltpu.CompilerParams(
            collective_id=0, has_side_effects=True, vmem_limit_bytes=int(53.85 * 1024 * 1024)
        ),
        cost_estimate=pl.CostEstimate(
            flops=2 * DEPTH * ROWS * HID, bytes_accessed=2 * DEPTH * HID, transcendentals=0
        ),
    )(tokens_in, grad_hidden)
    result = jnp.transpose(result, (0, 2, 1, 3)).reshape(2, 2, HID)
    return result[0], result[1]


def solution(mesh):
    placed = (P(("dp", "tensor"), None), P("dp", "tensor"))
    return jax.shard_map(
        local,
        mesh=mesh,
        in_specs=placed,
        out_specs=(P("dp", "tensor"), P("dp", "tensor")),
        check_vma=False,
    )
```

```python
import jax
import jax.numpy as jnp
from jax import lax
from jax.experimental import pallas as pl
from jax.experimental.pallas import tpu as pltpu
from jax.sharding import PartitionSpec as P

NY = 8
NZ = 8
NT = 4
TOKENS = 148
STEP = 144
SLOT = 160
DEPTH = 592
ROWS = 256
HALF = 128
HID = 4096
GROUP = 2048
EPS = 1e-06
F32 = jnp.float32
BF16 = jnp.bfloat16
MESH = pl.DeviceIdType.MESH
FAR_FIRST = (4, 3, 5, 2, 6, 1, 7)
RAW_TARGETS = (-4, -3, 3)
RAW_HOPS = (-2, -1, 1)
SUM_HOPS = (-2, 2, -1, 1)
RAW_PARTS = ((0, 1), (2,), (), ())


def row_order(group):
    new = lax.broadcasted_iota(jnp.int32, (ROWS, ROWS), 0)
    old = lax.broadcasted_iota(jnp.int32, (ROWS, ROWS), 1)
    core, first, second, i = new >> 7, (new >> 4) & 7, (new >> 1) & 7, new & 1
    y, z = (first, second) if group == 0 else (second, first)
    return jnp.where(old == 32 * y + 4 * z + 2 * core + i, 1.0, 0.0).astype(BF16)


def hadamard_pair():
    row = lax.broadcasted_iota(jnp.int32, (256, 256), 0)
    column = lax.broadcasted_iota(jnp.int32, (256, 256), 1)
    both = row & column & 127
    both = both ^ (both >> 4)
    both = both ^ (both >> 2)
    both = both ^ (both >> 1)
    sign = jnp.where((both & 1) == 0, 0.0625, -0.0625)
    return jnp.where((row >> 7) == (column >> 7), sign, 0.0).astype(BF16)


def kernel(
    tok_ref, grad_ref, out_ref,
    tok, shifted, order, table, slots, gbuf, turned, part, rot, other, squares,
    qall, qfirst, q1, q2, inv, ahead, land0, code, land1, acc, w, pack, land2,
    far, gsem, toksem, tsend, trecv, q1send, q1recv, q2send, q2recv, xsend, xrecv, send0, recv0,
    send1, recv1, send2, recv2,
):
    dp = lax.axis_index("dp")
    t = lax.axis_index("tensor")
    c = lax.rem(dp, 2)
    z = lax.rem(lax.div(dp, 2), NZ)
    y = lax.div(dp, 2 * NZ)
    oc = 1 - c

    def device(yy, zz, cc):
        return (yy * (2 * NZ) + zz * 2 + cc, t)

    def shift(value, k, n):
        return lax.rem(value + k, n)

    barrier = pltpu.get_barrier_semaphore()
    peers_t = [(dp, shift(t, k, NT)) for k in (1, 3)]
    peers_1 = [
        (kz * 2 + kc, shift(c, kc, 2), device(y, shift(z, kz, NZ), shift(c, kc, 2)))
        for kz in FAR_FIRST + (0,)
        for kc in (1, 0)
        if kz + kc > 0
    ]
    peers_y = [device(shift(y, k, NY), z, c) for k in range(1, NY)]

    def along(g, k, core):
        place = lax.rem(y + g * (z - y) + 8 + (1 - 2 * core) * k, 8)
        return place, (dp + (place - y - g * (z - y)) * (2 * NZ - 14 * g) + core - c, t)

    near = list(peers_t) + [(dp + oc - c, t)]
    for g in range(2):
        for k in (1, -1, 2, -2):
            near += [along(g, k, c)[1], along(g, k, oc)[1]]
    for peer in near:
        pl.semaphore_signal(barrier, inc=1, device_id=peer, device_id_type=MESH)
    tok_copy = pltpu.make_async_copy(tok_ref, tok, toksem)
    tok_copy.start()
    grad_copy = pltpu.make_async_copy(grad_ref, gbuf, gsem)
    grad_copy.start()
    shifted[...] = jnp.zeros((SLOT, ROWS), F32)
    tok_copy.wait()
    shifted[0:TOKENS, :] = tok[...].astype(F32)
    slots[0] = pltpu.roll(shifted[...], 4 * t, 0).astype(BF16)
    pl.semaphore_wait(barrier, len(near))

    def tokens(k):
        return pltpu.make_async_remote_copy(
            src_ref=slots.at[0], dst_ref=slots.at[k],
            send_sem=tsend.at[k], recv_sem=trecv.at[k],
            device_id=(dp, shift(t, k, NT)), device_id_type=MESH,
        )

    def pass_on(k):
        rows = pl.ds(0 if k == 1 else SLOT // 2, SLOT // 2)
        return pltpu.make_async_remote_copy(
            src_ref=slots.at[k, rows], dst_ref=slots.at[2, rows],
            send_sem=tsend.at[k - 1], recv_sem=trecv.at[k - 1],
            device_id=(dp, shift(t, k, NT)), device_id_type=MESH,
        )

    for k in (1, 3):
        tokens(k).start()
    for g in range(2):
        for k in (2, -2):
            pl.semaphore_signal(
                far, inc=1, device_id=along(g, k, c)[1], device_id_type=MESH
            )
    for g in range(2):
        order[g] = row_order(g)
    table[...] = hadamard_pair()
    for step, ks in enumerate(((0,), (1, 3), (2,))):
        if step == 1:
            for k in ks:
                tokens(k).wait_recv()
                pass_on(k).start()
        if step == 2:
            for k in (1, 3):
                pass_on(k).wait_recv()
        for n, k in enumerate(ks):
            features = slots[k]
            for g in range(2):
                turned[n, g] = lax.dot_general(
                    order[g], features, (((1,), (1,)), ((), ())),
                    preferred_element_type=F32,
                ).astype(BF16)
        if step == 0:
            grad_copy.wait()
        depths = [
            pl.ds(pl.multiple_of(shift(t, NT - k, NT) * STEP, 16), SLOT) for k in ks
        ]

        def columns(m, carry):
            g = m // 2 if step == 2 else lax.div(m, 2)
            total = None
            for tile in range(4):
                at = m * 1024 + tile * 256
                at = pl.ds(at if step == 2 else pl.multiple_of(at, 256), 256)
                value = part[:, at] if step > 0 else None
                for n, depth in enumerate(depths):
                    product = jnp.dot(
                        turned[n, g], gbuf[depth, at], preferred_element_type=F32
                    )
                    value = product if value is None else value + product
                part[:, at] = value
                if step == 2:
                    both = value * value
                    both = both[:, :128] + both[:, 128:]
                    total = both if total is None else total + both
            if step == 2:
                squares[m] = total
            return carry

        if step == 2:
            for m in range(4):
                columns(m, 0)
        else:
            lax.fori_loop(0, 4, columns, 0)

    def turn(value):
        high = value.astype(BF16)
        low = (value - high.astype(F32)).astype(BF16)
        return (
            jnp.dot(high, table[...], preferred_element_type=F32)
            + jnp.dot(low, table[...], preferred_element_type=F32)
        ).astype(BF16)

    def rotate(half, n):
        g, j = lax.div(n, 2), lax.rem(n, 2)
        rows = pl.ds(pl.multiple_of(half * HALF, HALF), HALF)
        value = jnp.concatenate(
            [
                part[rows, pl.ds(pl.multiple_of(n * 1024 + m * 256, 256), 256)]
                for m in range(4)
            ],
            axis=0,
        )
        result = turn(value)
        for m in range(4):
            at = pl.ds(pl.multiple_of(j * 1024 + m * 256, 256), 256)
            rot[g, rows, at] = result[m * HALF:(m + 1) * HALF]

    def cross(n):
        g, at = lax.div(n, 2), pl.ds(pl.multiple_of(lax.rem(n, 2) * 1024, 1024), 1024)
        return pltpu.make_async_remote_copy(
            src_ref=rot.at[g, pl.ds(pl.multiple_of(oc * HALF, HALF), HALF), at],
            dst_ref=other.at[g, :, at],
            send_sem=xsend.at[n], recv_sem=xrecv.at[n],
            device_id=device(y, z, oc), device_id_type=MESH,
        )

    def raw(g, other_core, j):
        core = shift(c, other_core, 2)
        n = other_core * 3 + j
        return pltpu.make_async_remote_copy(
            src_ref=ahead.at[g, n], dst_ref=land0.at[g, n],
            send_sem=send0.at[g, n], recv_sem=recv0.at[g, n],
            device_id=along(g, RAW_HOPS[j], core)[1], device_id_type=MESH,
        )

    def send_raw(js):
        chunks = [(j, g, n) for j in js for n in range(2) for g in range(2)]
        values = []
        for j, g, n in chunks:
            core = shift(c, n, 2)
            place = along(g, RAW_TARGETS[j], core)[0]
            rows = pl.ds(pl.multiple_of(core * HALF + place * 16, 16), 16)
            values += [
                part[rows, g * GROUP + m * 256:g * GROUP + (m + 1) * 256] for m in range(8)
            ]
        result = turn(jnp.concatenate(values, axis=0))
        for i, (j, g, n) in enumerate(chunks):
            for m in range(8):
                at = i * 128 + m * 16
                ahead[g, n * 3 + j, :, m * 256:(m + 1) * 256] = result[at:at + 16]
            raw(g, n, j).start()

    def rotate_theirs(g, carry):
        for j in range(2):
            rotate(oc, 2 * g + j)
            cross(2 * g + j).start()
        return carry

    def rotate_mine(g, carry):
        for j in range(2):
            rotate(c, 2 * g + j)
        return carry

    send_raw((0,))

    ones = jnp.ones((8, 128), F32)
    for g in range(2):
        q = lax.dot_general(
            ones, squares[2 * g] + squares[2 * g + 1], (((1,), (1,)), ((), ())),
            preferred_element_type=F32, precision=lax.Precision.HIGHEST,
        )
        for half in range(2):
            qall[half, g:g + 1, :] = q[0:1, half * HALF:(half + 1) * HALF]

    pl.semaphore_wait(far, 4)

    for slot, core, peer in peers_1:
        pltpu.make_async_remote_copy(
            src_ref=qall.at[core], dst_ref=q1.at[slot],
            send_sem=q1send, recv_sem=q1recv, device_id=peer, device_id_type=MESH,
        ).start()

    send_raw((1, 2))
    lax.fori_loop(0, 2, rotate_theirs, 0)

    q1_all = pltpu.make_async_remote_copy(
        src_ref=q1.at[pl.ds(1, 15)], dst_ref=q1.at[pl.ds(1, 15)],
        send_sem=q1send, recv_sem=q1recv, device_id=device(y, z, oc), device_id_type=MESH,
    )
    q1_all.wait_recv()
    best = qall[c]
    for slot in range(1, 16):
        best = jnp.maximum(best, q1[slot])
    qfirst[...] = best
    for k in FAR_FIRST:
        pltpu.make_async_remote_copy(
            src_ref=qfirst, dst_ref=q2.at[k],
            send_sem=q2send, recv_sem=q2recv, device_id=peers_y[k - 1], device_id_type=MESH,
        ).start()
    lax.fori_loop(0, 2, rotate_mine, 0)
    q2_all = pltpu.make_async_remote_copy(
        src_ref=q2.at[pl.ds(1, 7)], dst_ref=q2.at[pl.ds(1, 7)],
        send_sem=q2send, recv_sem=q2recv, device_id=peers_y[0], device_id_type=MESH,
    )
    q2_all.wait_recv()
    best = qfirst[...]
    for k in range(1, NY):
        best = jnp.maximum(best, q2[k])
    best = 0.7071067811865476 / jnp.sqrt(best / float(GROUP) + EPS)
    for g in range(2):
        inv[g] = jnp.transpose(jnp.broadcast_to(best[g:g + 1, :], (HALF, 128)))
    for n in range(4):
        cross(n).wait_recv()

    def coded(g, k, parts):
        place = along(g, k, c)[0]
        rows = pl.ds(pl.multiple_of(place * 16, 16), 16)
        mine = pl.ds(pl.multiple_of(c * HALF + place * 16, 16), 16)
        scale = jnp.concatenate([inv[g, rows, :]] * (GROUP // 128), axis=1)
        value = jnp.clip(rot[g, mine, :].astype(F32) * scale, -1.0, 1.0)
        value = value + jnp.clip(other[g, rows, :].astype(F32) * scale, -1.0, 1.0)
        for j in parts:
            for n in (j, 3 + j):
                value = value + jnp.clip(land0[g, n].astype(F32) * scale, -1.0, 1.0)
        return value

    def first(g, n):
        return pltpu.make_async_remote_copy(
            src_ref=code.at[g, n], dst_ref=land1.at[g, n],
            send_sem=send1.at[g, n], recv_sem=recv1.at[g, n],
            device_id=along(g, SUM_HOPS[n], c)[1], device_id_type=MESH,
        )

    def arrived(g, parts):
        for j in parts:
            for other_core in range(2):
                raw(g, other_core, j).wait_recv()

    for n in range(4):
        def send_sum(g, carry, n=n):
            arrived(g, RAW_PARTS[n])
            code[g, n] = coded(g, SUM_HOPS[n], RAW_PARTS[n]).astype(BF16)
            first(g, n).start()
            return carry

        lax.fori_loop(0, 2, send_sum, 0)

    def keep(g, carry):
        acc[g] = coded(g, 0, ())
        return carry

    lax.fori_loop(0, 2, keep, 0)

    def second(g, k):
        peer = device(y, shift(z, k, NZ), c) if g == 0 else device(shift(y, k, NY), z, c)
        return pltpu.make_async_remote_copy(
            src_ref=pack.at[g, shift((z, y)[g], k, 8)], dst_ref=land2.at[g, k],
            send_sem=send2.at[g, k], recv_sem=recv2.at[g, k],
            device_id=peer, device_id_type=MESH,
        )

    for g in range(2):
        value = acc[g]
        for n in (2, 3, 1, 0):
            first(g, n).wait_recv()
            value = value + land1[g, n].astype(F32)
        acc[g] = value
        for block in range(16):
            w[g, block * 16:(block + 1) * 16, :] = acc[g, :, block * 128:(block + 1) * 128]
        for place in range(8):
            pack[g, place] = jnp.concatenate(
                [w[g, pl.ds(place * 2 + i, 16, stride=16), :] for i in range(2)], axis=0
            ).astype(BF16)
        for k in FAR_FIRST:
            second(g, k).start()

    for k in (1, 3):
        tokens(k).wait_send()
        pass_on(k).wait_send()
    q1_all.wait_send()
    q2_all.wait_send()
    for g in range(2):
        for n in range(2):
            cross(2 * g + n).wait_send()
        for j in range(3):
            raw(g, 0, j).wait_send()
            raw(g, 1, j).wait_send()
        for n in range(4):
            first(g, n).wait_send()

    for g in range(2):
        total = pack[g, (z, y)[g]].astype(F32)
        for k in FAR_FIRST:
            second(g, k).wait_recv()
            total = total + land2[g, k].astype(F32)
        for i in range(2):
            row = (y, z)[g] * 16 + (z, y)[g] * 2 + i
            value = total[i * 16:(i + 1) * 16]
            at = g * 16
            scale = 1.4142135623730951 / inv[g, pl.ds(row, 1), :]
            out_ref[1, at:at + 16, i, :] = value
            out_ref[0, at:at + 16, i, :] = value * scale

    for g in range(2):
        for k in FAR_FIRST:
            second(g, k).wait_send()


def local(tokens_in, grad_hidden):
    dma = pltpu.SemaphoreType.DMA
    result = pl.pallas_call(
        kernel,
        out_shape=jax.ShapeDtypeStruct((2, 32, 2, 128), F32),
        in_specs=[pl.BlockSpec(memory_space=pl.ANY)] * 2,
        out_specs=pl.BlockSpec(memory_space=pltpu.VMEM),
        scratch_shapes=[
            pltpu.VMEM((TOKENS, ROWS), BF16),
            pltpu.VMEM((SLOT, ROWS), F32),
            pltpu.VMEM((2, 256, 256), BF16),
            pltpu.VMEM((256, 256), BF16),
            pltpu.VMEM((NT, SLOT, ROWS), BF16),
            pltpu.VMEM((DEPTH, HID), BF16),
            pltpu.VMEM((2, 2, ROWS, SLOT), BF16),
            pltpu.VMEM((ROWS, HID), F32),
            pltpu.VMEM((2, ROWS, GROUP), BF16),
            pltpu.VMEM((2, HALF, GROUP), BF16),
            pltpu.VMEM((4, ROWS, 128), F32),
            pltpu.VMEM((2, 2, 128), F32),
            pltpu.VMEM((2, 128), F32),
            pltpu.VMEM((16, 2, 128), F32),
            pltpu.VMEM((8, 2, 128), F32),
            pltpu.VMEM((2, HALF, 128), F32),
            pltpu.VMEM((2, 6, 16, GROUP), BF16),
            pltpu.VMEM((2, 6, 16, GROUP), BF16),
            pltpu.VMEM((2, 4, 16, GROUP), BF16),
            pltpu.VMEM((2, 4, 16, GROUP), BF16),
            pltpu.VMEM((2, 16, GROUP), F32),
            pltpu.VMEM((2, 256, 128), F32),
            pltpu.VMEM((2, 8, 32, 128), BF16),
            pltpu.VMEM((2, 8, 32, 128), BF16),
            pltpu.SemaphoreType.REGULAR, dma, dma, dma((NT,)), dma((NT,)), dma, dma, dma, dma, dma((4,)), dma((4,)),
            dma((2, 6)), dma((2, 6)), dma((2, 4)), dma((2, 4)), dma((2, 8)), dma((2, 8)),
        ],
        compiler_params=pltpu.CompilerParams(
            collective_id=0, has_side_effects=True, vmem_limit_bytes=int(53.85 * 1024 * 1024)
        ),
        cost_estimate=pl.CostEstimate(
            flops=2 * DEPTH * ROWS * HID, bytes_accessed=2 * DEPTH * HID, transcendentals=0
        ),
    )(tokens_in, grad_hidden)
    result = jnp.transpose(result, (0, 2, 1, 3)).reshape(2, 2, HID)
    return result[0], result[1]


def solution(mesh):
    placed = (P(("dp", "tensor"), None), P("dp", "tensor"))
    return jax.shard_map(
        local,
        mesh=mesh,
        in_specs=placed,
        out_specs=(P("dp", "tensor"), P("dp", "tensor")),
        check_vma=False,
    )
```

```python
import jax
import jax.numpy as jnp
from jax import lax
from jax.experimental import pallas as pl
from jax.experimental.pallas import tpu as pltpu
from jax.sharding import PartitionSpec as P

NY = 8
NZ = 8
NT = 4
TOKENS = 148
STEP = 144
SLOT = 160
DEPTH = 592
ROWS = 256
HALF = 128
HID = 4096
GROUP = 2048
EPS = 1e-06
F32 = jnp.float32
BF16 = jnp.bfloat16
MESH = pl.DeviceIdType.MESH
FAR_FIRST = (4, 3, 5, 2, 6, 1, 7)
RAW_TARGETS = (-4, -3, 3)
RAW_HOPS = (-2, -1, 1)
SUM_HOPS = (-2, 2, -1, 1)
RAW_PARTS = ((0, 1), (2,), (), ())


def row_order(group):
    new = lax.broadcasted_iota(jnp.int32, (ROWS, ROWS), 0)
    old = lax.broadcasted_iota(jnp.int32, (ROWS, ROWS), 1)
    core, first, second, i = new >> 7, (new >> 4) & 7, (new >> 1) & 7, new & 1
    y, z = (first, second) if group == 0 else (second, first)
    return jnp.where(old == 32 * y + 4 * z + 2 * core + i, 1.0, 0.0).astype(BF16)


def hadamard_pair():
    row = lax.broadcasted_iota(jnp.int32, (256, 256), 0)
    column = lax.broadcasted_iota(jnp.int32, (256, 256), 1)
    both = row & column & 127
    both = both ^ (both >> 4)
    both = both ^ (both >> 2)
    both = both ^ (both >> 1)
    sign = jnp.where((both & 1) == 0, 0.0625, -0.0625)
    return jnp.where((row >> 7) == (column >> 7), sign, 0.0).astype(BF16)


def kernel(
    tok_ref, grad_ref, out_ref,
    tok, shifted, order, table, slots, gbuf, turned, part, rot, other, squares,
    qall, qfirst, q1, q2, inv, ahead, land0, code, land1, acc, w, pack, land2,
    far, gsem, toksem, tsend, trecv, q1send, q1recv, q2send, q2recv, xsend, xrecv, send0, recv0,
    send1, recv1, send2, recv2,
):
    dp = lax.axis_index("dp")
    t = lax.axis_index("tensor")
    c = lax.rem(dp, 2)
    z = lax.rem(lax.div(dp, 2), NZ)
    y = lax.div(dp, 2 * NZ)
    oc = 1 - c

    def device(yy, zz, cc):
        return (yy * (2 * NZ) + zz * 2 + cc, t)

    def shift(value, k, n):
        return lax.rem(value + k, n)

    barrier = pltpu.get_barrier_semaphore()
    peers_t = [(dp, shift(t, k, NT)) for k in (1, 3)]
    peers_1 = [
        (kz * 2 + kc, shift(c, kc, 2), device(y, shift(z, kz, NZ), shift(c, kc, 2)))
        for kz in FAR_FIRST + (0,)
        for kc in (1, 0)
        if kz + kc > 0
    ]
    peers_y = [device(shift(y, k, NY), z, c) for k in range(1, NY)]

    def along(g, k, core):
        place = lax.rem(y + g * (z - y) + 8 + (1 - 2 * core) * k, 8)
        return place, (dp + (place - y - g * (z - y)) * (2 * NZ - 14 * g) + core - c, t)

    near = list(peers_t) + [(dp + oc - c, t)]
    for g in range(2):
        for k in (1, -1, 2, -2):
            near += [along(g, k, c)[1], along(g, k, oc)[1]]
    for peer in near:
        pl.semaphore_signal(barrier, inc=1, device_id=peer, device_id_type=MESH)
    tok_copy = pltpu.make_async_copy(tok_ref, tok, toksem)
    tok_copy.start()
    grad_copy = pltpu.make_async_copy(grad_ref, gbuf, gsem)
    grad_copy.start()
    shifted[...] = jnp.zeros((SLOT, ROWS), F32)
    tok_copy.wait()
    shifted[0:TOKENS, :] = tok[...].astype(F32)
    slots[0] = pltpu.roll(shifted[...], 4 * t, 0).astype(BF16)
    pl.semaphore_wait(barrier, len(near))

    def tokens(k):
        return pltpu.make_async_remote_copy(
            src_ref=slots.at[0], dst_ref=slots.at[k],
            send_sem=tsend.at[k], recv_sem=trecv.at[k],
            device_id=(dp, shift(t, k, NT)), device_id_type=MESH,
        )

    def pass_on(k):
        rows = pl.ds(0 if k == 1 else SLOT // 2, SLOT // 2)
        return pltpu.make_async_remote_copy(
            src_ref=slots.at[k, rows], dst_ref=slots.at[2, rows],
            send_sem=tsend.at[k - 1], recv_sem=trecv.at[k - 1],
            device_id=(dp, shift(t, k, NT)), device_id_type=MESH,
        )

    for k in (1, 3):
        tokens(k).start()
    for g in range(2):
        for k in (2, -2):
            pl.semaphore_signal(
                far, inc=1, device_id=along(g, k, c)[1], device_id_type=MESH
            )
    for g in range(2):
        order[g] = row_order(g)
    table[...] = hadamard_pair()
    for step, ks in enumerate(((0,), (1, 3), (2,))):
        if step == 1:
            for k in ks:
                tokens(k).wait_recv()
                pass_on(k).start()
        if step == 2:
            for k in (1, 3):
                pass_on(k).wait_recv()
        for n, k in enumerate(ks):
            features = slots[k]
            for g in range(2):
                turned[n, g] = lax.dot_general(
                    order[g], features, (((1,), (1,)), ((), ())),
                    preferred_element_type=F32,
                ).astype(BF16)
        if step == 0:
            grad_copy.wait()
        depths = [
            pl.ds(pl.multiple_of(shift(t, NT - k, NT) * STEP, 16), SLOT) for k in ks
        ]

        def columns(m, carry):
            g = m // 2 if step == 2 else lax.div(m, 2)
            total = None
            for tile in range(4):
                at = m * 1024 + tile * 256
                at = pl.ds(at if step == 2 else pl.multiple_of(at, 256), 256)
                value = part[:, at] if step > 0 else None
                for n, depth in enumerate(depths):
                    product = jnp.dot(
                        turned[n, g], gbuf[depth, at], preferred_element_type=F32
                    )
                    value = product if value is None else value + product
                part[:, at] = value
                if step == 2:
                    both = value * value
                    both = both[:, :128] + both[:, 128:]
                    total = both if total is None else total + both
            if step == 2:
                squares[m] = total
            return carry

        if step == 2:
            for m in range(4):
                columns(m, 0)
        else:
            lax.fori_loop(0, 4, columns, 0)

    def turn(value):
        high = value.astype(BF16)
        low = (value - high.astype(F32)).astype(BF16)
        return (
            jnp.dot(high, table[...], preferred_element_type=F32)
            + jnp.dot(low, table[...], preferred_element_type=F32)
        ).astype(BF16)

    def rotate(half, n):
        g, j = lax.div(n, 2), lax.rem(n, 2)
        rows = pl.ds(pl.multiple_of(half * HALF, HALF), HALF)
        value = jnp.concatenate(
            [
                part[rows, pl.ds(pl.multiple_of(n * 1024 + m * 256, 256), 256)]
                for m in range(4)
            ],
            axis=0,
        )
        result = turn(value)
        for m in range(4):
            at = pl.ds(pl.multiple_of(j * 1024 + m * 256, 256), 256)
            rot[g, rows, at] = result[m * HALF:(m + 1) * HALF]

    def cross(n):
        g, at = lax.div(n, 2), pl.ds(pl.multiple_of(lax.rem(n, 2) * 1024, 1024), 1024)
        return pltpu.make_async_remote_copy(
            src_ref=rot.at[g, pl.ds(pl.multiple_of(oc * HALF, HALF), HALF), at],
            dst_ref=other.at[g, :, at],
            send_sem=xsend.at[n], recv_sem=xrecv.at[n],
            device_id=device(y, z, oc), device_id_type=MESH,
        )

    def raw(g, other_core, j):
        core = shift(c, other_core, 2)
        n = other_core * 3 + j
        return pltpu.make_async_remote_copy(
            src_ref=ahead.at[g, n], dst_ref=land0.at[g, n],
            send_sem=send0.at[g, n], recv_sem=recv0.at[g, n],
            device_id=along(g, RAW_HOPS[j], core)[1], device_id_type=MESH,
        )

    def send_raw(js):
        chunks = [(j, g, n) for j in js for n in range(2) for g in range(2)]
        values = []
        for j, g, n in chunks:
            core = shift(c, n, 2)
            place = along(g, RAW_TARGETS[j], core)[0]
            rows = pl.ds(pl.multiple_of(core * HALF + place * 16, 16), 16)
            values += [
                part[rows, g * GROUP + m * 256:g * GROUP + (m + 1) * 256] for m in range(8)
            ]
        result = turn(jnp.concatenate(values, axis=0))
        for i, (j, g, n) in enumerate(chunks):
            for m in range(8):
                at = i * 128 + m * 16
                ahead[g, n * 3 + j, :, m * 256:(m + 1) * 256] = result[at:at + 16]
            raw(g, n, j).start()

    def rotate_theirs(g, carry):
        for j in range(2):
            rotate(oc, 2 * g + j)
            cross(2 * g + j).start()
        return carry

    def rotate_mine(g, carry):
        for j in range(2):
            rotate(c, 2 * g + j)
        return carry

    ones = jnp.ones((8, 128), F32)
    for g in range(2):
        q = lax.dot_general(
            ones, squares[2 * g] + squares[2 * g + 1], (((1,), (1,)), ((), ())),
            preferred_element_type=F32, precision=lax.Precision.HIGHEST,
        )
        for half in range(2):
            qall[half, g:g + 1, :] = q[0:1, half * HALF:(half + 1) * HALF]

    pl.semaphore_wait(far, 4)

    for slot, core, peer in peers_1:
        pltpu.make_async_remote_copy(
            src_ref=qall.at[core], dst_ref=q1.at[slot],
            send_sem=q1send, recv_sem=q1recv, device_id=peer, device_id_type=MESH,
        ).start()

    send_raw((0,))
    send_raw((1, 2))
    lax.fori_loop(0, 2, rotate_theirs, 0)

    q1_all = pltpu.make_async_remote_copy(
        src_ref=q1.at[pl.ds(1, 15)], dst_ref=q1.at[pl.ds(1, 15)],
        send_sem=q1send, recv_sem=q1recv, device_id=device(y, z, oc), device_id_type=MESH,
    )
    q1_all.wait_recv()
    best = qall[c]
    for slot in range(1, 16):
        best = jnp.maximum(best, q1[slot])
    qfirst[...] = best
    for k in FAR_FIRST:
        pltpu.make_async_remote_copy(
            src_ref=qfirst, dst_ref=q2.at[k],
            send_sem=q2send, recv_sem=q2recv, device_id=peers_y[k - 1], device_id_type=MESH,
        ).start()
    lax.fori_loop(0, 2, rotate_mine, 0)
    q2_all = pltpu.make_async_remote_copy(
        src_ref=q2.at[pl.ds(1, 7)], dst_ref=q2.at[pl.ds(1, 7)],
        send_sem=q2send, recv_sem=q2recv, device_id=peers_y[0], device_id_type=MESH,
    )
    q2_all.wait_recv()
    best = qfirst[...]
    for k in range(1, NY):
        best = jnp.maximum(best, q2[k])
    best = 0.7071067811865476 / jnp.sqrt(best / float(GROUP) + EPS)
    for g in range(2):
        inv[g] = jnp.transpose(jnp.broadcast_to(best[g:g + 1, :], (HALF, 128)))
    for n in range(4):
        cross(n).wait_recv()

    def coded(g, k, parts):
        place = along(g, k, c)[0]
        rows = pl.ds(pl.multiple_of(place * 16, 16), 16)
        mine = pl.ds(pl.multiple_of(c * HALF + place * 16, 16), 16)
        scale = jnp.concatenate([inv[g, rows, :]] * (GROUP // 128), axis=1)
        value = jnp.clip(rot[g, mine, :].astype(F32) * scale, -1.0, 1.0)
        value = value + jnp.clip(other[g, rows, :].astype(F32) * scale, -1.0, 1.0)
        for j in parts:
            for n in (j, 3 + j):
                value = value + jnp.clip(land0[g, n].astype(F32) * scale, -1.0, 1.0)
        return value

    def first(g, n):
        return pltpu.make_async_remote_copy(
            src_ref=code.at[g, n], dst_ref=land1.at[g, n],
            send_sem=send1.at[g, n], recv_sem=recv1.at[g, n],
            device_id=along(g, SUM_HOPS[n], c)[1], device_id_type=MESH,
        )

    def arrived(g, parts):
        for j in parts:
            for other_core in range(2):
                raw(g, other_core, j).wait_recv()

    for n in range(4):
        def send_sum(g, carry, n=n):
            arrived(g, RAW_PARTS[n])
            code[g, n] = coded(g, SUM_HOPS[n], RAW_PARTS[n]).astype(BF16)
            first(g, n).start()
            return carry

        lax.fori_loop(0, 2, send_sum, 0)

    def keep(g, carry):
        acc[g] = coded(g, 0, ())
        return carry

    lax.fori_loop(0, 2, keep, 0)

    def second(g, k):
        peer = device(y, shift(z, k, NZ), c) if g == 0 else device(shift(y, k, NY), z, c)
        return pltpu.make_async_remote_copy(
            src_ref=pack.at[g, shift((z, y)[g], k, 8)], dst_ref=land2.at[g, k],
            send_sem=send2.at[g, k], recv_sem=recv2.at[g, k],
            device_id=peer, device_id_type=MESH,
        )

    for g in range(2):
        value = acc[g]
        for n in (2, 3, 1, 0):
            first(g, n).wait_recv()
            value = value + land1[g, n].astype(F32)
        acc[g] = value
        for block in range(16):
            w[g, block * 16:(block + 1) * 16, :] = acc[g, :, block * 128:(block + 1) * 128]
        for place in range(8):
            pack[g, place] = jnp.concatenate(
                [w[g, pl.ds(place * 2 + i, 16, stride=16), :] for i in range(2)], axis=0
            ).astype(BF16)
        for k in FAR_FIRST:
            second(g, k).start()

    for k in (1, 3):
        tokens(k).wait_send()
        pass_on(k).wait_send()
    q1_all.wait_send()
    q2_all.wait_send()
    for g in range(2):
        for n in range(2):
            cross(2 * g + n).wait_send()
        for j in range(3):
            raw(g, 0, j).wait_send()
            raw(g, 1, j).wait_send()
        for n in range(4):
            first(g, n).wait_send()

    for g in range(2):
        total = pack[g, (z, y)[g]].astype(F32)
        for k in FAR_FIRST:
            second(g, k).wait_recv()
            total = total + land2[g, k].astype(F32)
        for i in range(2):
            row = (y, z)[g] * 16 + (z, y)[g] * 2 + i
            value = total[i * 16:(i + 1) * 16]
            at = g * 16
            scale = 1.4142135623730951 / inv[g, pl.ds(row, 1), :]
            out_ref[1, at:at + 16, i, :] = value
            out_ref[0, at:at + 16, i, :] = value * scale

    for g in range(2):
        for k in FAR_FIRST:
            second(g, k).wait_send()


def local(tokens_in, grad_hidden):
    dma = pltpu.SemaphoreType.DMA
    result = pl.pallas_call(
        kernel,
        out_shape=jax.ShapeDtypeStruct((2, 32, 2, 128), F32),
        in_specs=[pl.BlockSpec(memory_space=pl.ANY)] * 2,
        out_specs=pl.BlockSpec(memory_space=pltpu.VMEM),
        scratch_shapes=[
            pltpu.VMEM((TOKENS, ROWS), BF16),
            pltpu.VMEM((SLOT, ROWS), F32),
            pltpu.VMEM((2, 256, 256), BF16),
            pltpu.VMEM((256, 256), BF16),
            pltpu.VMEM((NT, SLOT, ROWS), BF16),
            pltpu.VMEM((DEPTH, HID), BF16),
            pltpu.VMEM((2, 2, ROWS, SLOT), BF16),
            pltpu.VMEM((ROWS, HID), F32),
            pltpu.VMEM((2, ROWS, GROUP), BF16),
            pltpu.VMEM((2, HALF, GROUP), BF16),
            pltpu.VMEM((4, ROWS, 128), F32),
            pltpu.VMEM((2, 2, 128), F32),
            pltpu.VMEM((2, 128), F32),
            pltpu.VMEM((16, 2, 128), F32),
            pltpu.VMEM((8, 2, 128), F32),
            pltpu.VMEM((2, HALF, 128), F32),
            pltpu.VMEM((2, 6, 16, GROUP), BF16),
            pltpu.VMEM((2, 6, 16, GROUP), BF16),
            pltpu.VMEM((2, 4, 16, GROUP), BF16),
            pltpu.VMEM((2, 4, 16, GROUP), BF16),
            pltpu.VMEM((2, 16, GROUP), F32),
            pltpu.VMEM((2, 256, 128), F32),
            pltpu.VMEM((2, 8, 32, 128), BF16),
            pltpu.VMEM((2, 8, 32, 128), BF16),
            pltpu.SemaphoreType.REGULAR, dma, dma, dma((NT,)), dma((NT,)), dma, dma, dma, dma, dma((4,)), dma((4,)),
            dma((2, 6)), dma((2, 6)), dma((2, 4)), dma((2, 4)), dma((2, 8)), dma((2, 8)),
        ],
        compiler_params=pltpu.CompilerParams(
            collective_id=0, has_side_effects=True, vmem_limit_bytes=int(53.85 * 1024 * 1024)
        ),
        cost_estimate=pl.CostEstimate(
            flops=2 * DEPTH * ROWS * HID, bytes_accessed=2 * DEPTH * HID, transcendentals=0
        ),
    )(tokens_in, grad_hidden)
    result = jnp.transpose(result, (0, 2, 1, 3)).reshape(2, 2, HID)
    return result[0], result[1]


def solution(mesh):
    placed = (P(("dp", "tensor"), None), P("dp", "tensor"))
    return jax.shard_map(
        local,
        mesh=mesh,
        in_specs=placed,
        out_specs=(P("dp", "tensor"), P("dp", "tensor")),
        check_vma=False,
    )
```
